32 devices in a mesh: row: 8 (over y, x, core), col: 4 (over z).
Axes of the slice: x: 2, y: 2, z: 4, core: 2. Of those that a mesh axis runs over, the one named last changes fastest.
Arguments:
- a_tiles: bfloat16 [4096, 128, 128], P(('row', 'col')), may hold values from -6 to 6
- a_row: int32 [4096], P(('row', 'col')), may hold values from 0 to 15
- a_col: int32 [4096], P(('row', 'col')), may hold values from 0 to 11
- a_count: int32 [32], P(('row', 'col')), may hold values from 32 to 128
- p_tiles: bfloat16 [128, 128, 128], P(('row', 'col')), may hold values from -0.5 to 0.5
Outputs:
- coarse_tiles: bfloat16 [384, 128, 128], P(('row', 'col'))
The draws below stay inside these ranges and needn't reach their ends.
All inputs are finite; a program needn't handle non-finite values.
Results may differ from the reference program's by a relative error of at most 0.0049.
Values may be sent and summed in bfloat16 or wider, within the bound.
No kernel may reach another device: no remote copies, remote signals or barrier semaphores. Data moves between devices by JAX's collectives and lax.ppermute only.
A program may use at most 64 MiB of HBM per device.

```python
import jax
import jax.numpy as jnp
from jax import lax

TILE = 128
PB = 4
TD = 128
CT = 12
NB = 128
N_ROW = 8
N_COL = 4


def draw_a_row(key, part):
    total = N_ROW * N_COL * TD
    upper = N_COL * PB
    values = jax.random.randint(jax.random.fold_in(key, 11), (total,), 0, upper)
    values = values.at[0].set(upper - 1).at[1].set(0)
    return values.astype(jnp.int32)


def draw_a_col(key, part):
    total = N_ROW * N_COL * TD
    upper = 3 * PB
    values = jax.random.randint(jax.random.fold_in(key, 12), (total,), 0, upper)
    values = values.at[0].set(upper - 1).at[1].set(0)
    return values.astype(jnp.int32)


def draw_a_count(key, part):
    divisor = 1 + jax.random.randint(jax.random.fold_in(key, 14), (N_ROW * N_COL,), 0, 4)
    counts = TD // divisor
    counts = counts.at[0].set(TD).at[1].set(TD // 4)
    return counts.astype(jnp.int32)


def steps_of(key, dims, split, least, high):
    loudness, own = 1.0, jax.random.fold_in(key, 6)
    for position, parts in split:
        steps = jnp.exp(jax.random.uniform(jax.random.fold_in(own, position), (parts,), jnp.float32, least / len(split), high / len(split)))
        loudness = loudness * jnp.repeat(steps, dims[position] // parts).reshape([-1 if axis == position else 1 for axis in range(len(dims))])
    return loudness


def noise(key, extent, spread, most, split=(), kind=jnp.bfloat16):
    drawn = spread * jax.random.normal(key, extent, jnp.float32)
    if split:
        drawn = drawn * steps_of(key, extent, split, -0.22, 0.18)
    return jnp.clip(drawn, -most, most).astype(kind)


def setup_inputs(seed: int = 0) -> dict:
    keys = jax.random.split(jax.random.key(seed), 6)
    a_tiles = noise(keys[0], (N_ROW * N_COL * TD, TILE, TILE), 1.0, 6.0, ((0, 32),))
    a_row = draw_a_row(jax.random.fold_in(keys[5], 71), 0)
    a_col = draw_a_col(jax.random.fold_in(keys[5], 71), 0)
    a_count = draw_a_count(jax.random.fold_in(keys[5], 71), 0)
    p_tiles = noise(keys[4], (NB, TILE, TILE), TILE ** -0.5, 0.5, ((0, 32),))
    return dict(a_tiles=a_tiles, a_row=a_row, a_col=a_col, a_count=a_count, p_tiles=p_tiles)


def reference(a_tiles, a_row, a_col, a_count, p_tiles):
    blocks = p_tiles.reshape(N_ROW, N_COL, PB, TILE, TILE)
    coarse_total = 3 * PB * PB

    def group_sum(row_index):
        row_side = lax.dynamic_index_in_dim(blocks, row_index, 0, keepdims=False).reshape(N_COL * PB, TILE, TILE)

        def one_device(col_index, total):
            device = (row_index * N_COL + col_index).astype(jnp.int32)
            neighbours = []
            for shift_value in (-1, 0, 1):
                other = ((row_index + shift_value + N_ROW) % N_ROW).astype(jnp.int32)
                group = lax.dynamic_index_in_dim(blocks, other, 0, keepdims=False)
                neighbours.append(lax.dynamic_index_in_dim(group, col_index.astype(jnp.int32), 0, keepdims=False))
            col_side = jnp.concatenate(neighbours, axis=0)
            start = (device * TD).astype(jnp.int32)
            tiles = lax.dynamic_slice_in_dim(a_tiles, start, TD, 0)
            rows = lax.dynamic_slice_in_dim(a_row, start, TD, 0)
            cols = lax.dynamic_slice_in_dim(a_col, start, TD, 0)
            count = lax.dynamic_index_in_dim(a_count, device, 0, keepdims=False)
            is_live = jnp.arange(TD, dtype=jnp.int32) < count
            slots = ((rows % PB) * (3 * PB) + cols).astype(jnp.int32)
            right = col_side[cols]
            image = jnp.einsum("tij,tjk->tik", tiles.astype(jnp.float32), right.astype(jnp.float32)).astype(jnp.bfloat16)
            left = row_side[rows]
            terms = jnp.einsum("tji,tjk->tik", left.astype(jnp.float32), image.astype(jnp.float32))
            terms = jnp.where(is_live[:, None, None], terms, jnp.float32(0.0))
            return total.at[slots].add(terms)

        empty = jnp.zeros((coarse_total, TILE, TILE), jnp.float32)
        total = lax.fori_loop(jnp.int32(0), jnp.int32(N_COL), one_device, empty)
        return total.astype(jnp.bfloat16)

    result = lax.map(group_sum, jnp.arange(N_ROW, dtype=jnp.int32))
    return result.reshape(N_ROW * N_COL * CT, TILE, TILE)
```

```python
import functools

import jax
import jax.numpy as jnp
from jax import lax
from jax.experimental import pallas as pl
from jax.experimental.pallas import tpu as pltpu
from jax.sharding import PartitionSpec as P

UNROLL = 4
LIMIT = 40 * 1024 * 1024
VMEM = pl.BlockSpec(memory_space=pltpu.VMEM)
SMEM = pl.BlockSpec(memory_space=pltpu.SMEM)


def bits(extent):
    return (extent - 1).bit_length()


def plan_kernel(held, chunk, a_row, a_col, a_count, items, counts):
    slots, n = a_row.shape[0], counts.shape[0]
    for d in range(n):
        counts[d] = 0

    def place(t, carry):
        row, col = a_row[t], a_col[t]
        place = row % held * (3 * held) + col
        d = place // chunk
        at = counts[d]
        item = (row << bits(3 * held)) + col
        item = (item << bits(chunk)) + place - d * chunk
        items[d * slots + at] = (item << bits(slots)) + t
        counts[d] = at + 1
        return carry

    lax.fori_loop(0, a_count[0], place, 0)


def plan(held, chunk, n, a_row, a_col, a_count):
    return pl.pallas_call(
        functools.partial(plan_kernel, held, chunk),
        out_shape=(
            jax.ShapeDtypeStruct((n * a_row.shape[0],), jnp.int32),
            jax.ShapeDtypeStruct((n,), jnp.int32),
        ),
        in_specs=[SMEM] * 3,
        out_specs=(SMEM, SMEM),
        name="plan",
    )(a_row, a_col, a_count)


def chunk_kernel(held, chunk, n_right, n_left, dest, items, counts, a, *rest):
    rights, lefts = rest[:n_right], rest[n_right : n_right + n_left]
    out, right, left, accum = rest[n_right + n_left :]
    slots = a.shape[0]
    d = dest[0]
    base, count = d * slots, counts[d]
    for i in range(n_right):
        right[i * held : (i + 1) * held] = rights[i][...]
    at = 0
    for ref in lefts:
        for i in range(ref.shape[0]):
            left[at] = ref[i].T
            at += 1
    accum[...] = jnp.zeros_like(accum)

    def advance(step, carry):
        for u in range(UNROLL):
            e = step * UNROLL + u
            item = items[base + jnp.minimum(e, count - 1)]
            t, item = item & ((1 << bits(slots)) - 1), item >> bits(slots)
            s, item = item & ((1 << bits(chunk)) - 1), item >> bits(chunk)
            col, row = item & ((1 << bits(3 * held)) - 1), item >> bits(3 * held)
            s = jnp.where(e < count, s, chunk)
            image = jnp.dot(a[t], right[col], preferred_element_type=jnp.float32)
            accum[s] += jnp.dot(
                left[row], image.astype(jnp.bfloat16), preferred_element_type=jnp.float32
            )
        return carry

    lax.fori_loop(0, (count + UNROLL - 1) // UNROLL, advance, 0)
    out[...] = accum[:chunk].astype(out.dtype)


def coarse_chunk(held, chunk, dest, items, counts, a, rights, lefts, dtype):
    width = a.shape[1]
    n_left = sum(x.shape[0] for x in lefts)
    return pl.pallas_call(
        functools.partial(chunk_kernel, held, chunk, len(rights), len(lefts)),
        out_shape=jax.ShapeDtypeStruct((chunk, width, width), dtype),
        in_specs=[SMEM] * 3 + [VMEM] * (1 + len(rights) + len(lefts)),
        out_specs=VMEM,
        scratch_shapes=[
            pltpu.VMEM((3 * held, width, width), jnp.bfloat16),
            pltpu.VMEM((n_left, width, width), jnp.bfloat16),
            pltpu.VMEM((chunk + 1, width, width), jnp.float32),
        ],
        compiler_params=pltpu.CompilerParams(vmem_limit_bytes=LIMIT),
        name="coarse_chunk",
    )(dest, items, counts, a, *rights, *lefts)


def shifted(block, axis, distance):
    n = lax.axis_size(axis)
    return lax.ppermute(block, axis, [((i - distance) % n, i) for i in range(n)])


def shards(a_tiles, a_row, a_col, a_count, p_tiles):
    n, me = lax.axis_size("col"), lax.axis_index("col")
    held = p_tiles.shape[0]
    total = 3 * held * held
    chunk = total // n
    rights = [shifted(p_tiles, "row", 1), p_tiles, shifted(p_tiles, "row", -1)]
    row_side = lax.all_gather(p_tiles, "col", axis=0, tiled=True)
    items, counts = plan(held, total, 1, a_row, a_col, a_count)
    zero = jnp.zeros((1,), jnp.int32)
    sums = coarse_chunk(held, total, zero, items, counts, a_tiles, rights, [row_side], jnp.bfloat16)
    parts = sums.reshape(n, chunk, *sums.shape[1:])
    parts = lax.all_to_all(parts, "col", 0, 0, tiled=True)
    return jnp.sum(parts.astype(jnp.float32), axis=0).astype(jnp.bfloat16)


def solution(mesh):
    in_specs = (
        P(("row", "col"), None, None),
        P(("row", "col")),
        P(("row", "col")),
        P(("row", "col")),
        P(("row", "col"), None, None),
    )
    out_specs = P(("row", "col"), None, None)
    return jax.shard_map(shards, mesh=mesh, in_specs=in_specs, out_specs=out_specs, check_vma=False)
```

```python
import functools

import jax
import jax.numpy as jnp
from jax import lax
from jax.experimental import pallas as pl
from jax.experimental.pallas import tpu as pltpu
from jax.sharding import PartitionSpec as P

UNROLLS = (16, 4)
LIMIT = 12 * 1024 * 1024
VMEM = pl.BlockSpec(memory_space=pltpu.VMEM)
SMEM = pl.BlockSpec(memory_space=pltpu.SMEM)
HBM = pl.BlockSpec(memory_space=pltpu.HBM)


def bits(extent):
    return (extent - 1).bit_length()


def divide(x, n):
    if n & (n - 1):
        return lax.div(x, n), lax.rem(x, n)
    return x >> bits(n), x & (n - 1)


def plan_kernel(held, n, me, a_row, a_col, a_count, a, p, items, counts, a_out, p_out, sems):
    slots = a_row.shape[0]
    copies = [pltpu.make_async_copy(p, p_out, sems.at[0]), pltpu.make_async_copy(a, a_out, sems.at[1])]
    for copy in copies:
        copy.start()
    field = 32 // n
    group = 8 if slots % 8 == 0 else 1
    live = a_count[0]

    def place(step, taken):
        for u in range(group):
            t = step * group + u
            row, col = a_row[t], a_col[t]
            d = divide(divide(row, held)[1] * n, held)[0]
            at = (taken >> (d * field)) & ((1 << min(field, 16)) - 1)
            items[d * slots + at] = t + (col << bits(slots)) + (row << (bits(slots) + bits(3 * held)))
            taken = taken + (jnp.where(t < live, 1, 0) << (d * field))
        return taken

    taken = lax.fori_loop(0, lax.div(live + group - 1, group), place, jnp.int32(0))
    for d in range(n):
        counts[d] = (taken >> (d * field)) & ((1 << min(field, 16)) - 1)
    counts[n] = me[0]
    for copy in copies:
        copy.wait()


def plan(held, n, me, a_row, a_col, a_count, a_tiles, p_tiles):
    return pl.pallas_call(
        functools.partial(plan_kernel, held, n),
        out_shape=(
            jax.ShapeDtypeStruct((n * a_row.shape[0],), jnp.int32),
            jax.ShapeDtypeStruct((n + 1,), jnp.int32),
            pltpu.VMEM(a_tiles.shape, a_tiles.dtype),
            pltpu.VMEM(p_tiles.shape, p_tiles.dtype),
        ),
        in_specs=[SMEM] * 4 + [HBM] * 2,
        out_specs=(SMEM, SMEM, VMEM, VMEM),
        scratch_shapes=[pltpu.SemaphoreType.DMA((2,))],
        compiler_params=pltpu.CompilerParams(vmem_limit_bytes=LIMIT),
        name="plan",
    )(me, a_row, a_col, a_count, a_tiles, p_tiles)


def chunk_kernel(held, flip, n_left, n_out, items, counts, a, below, own, above, *rest):
    lefts, outs, (right, left, accum) = rest[:n_left], rest[-3 - n_out : -3], rest[-3:]
    slots, chunk = a.shape[0], outs[0].shape[0]
    me = counts[counts.shape[0] - 1]
    d = 0 if flip is None else me ^ flip
    base, count = d * slots, counts[d]
    for i, ref in enumerate((below, own, above)):
        right[i * held : (i + 1) * held] = ref[...]
    if flip is None:
        for i in range(left.shape[0]):
            left[i] = lefts[0][i].T
    else:
        for i in range(n_left):
            left[i] = lefts[i][d].T
    accum[...] = jnp.zeros_like(accum)

    def take(e):
        item = items[base + jnp.minimum(e, count - 1)]
        t, item = item & ((1 << bits(slots)) - 1), item >> bits(slots)
        col, row = item & ((1 << bits(3 * held)) - 1), item >> bits(3 * held)
        if flip is None:
            s = divide(row, held)[1] * (3 * held) + col
        else:
            row, s = divide(row, held)[0] ^ me, col
        s = jnp.where(e < count, s, chunk)
        image = jnp.dot(a[t], right[col], preferred_element_type=jnp.float32)
        accum[s] += jnp.dot(left[row], image.astype(jnp.bfloat16), preferred_element_type=jnp.float32)

    done = jnp.int32(0)
    for unroll in UNROLLS:

        def advance(step, carry, done=done, unroll=unroll):
            for u in range(unroll):
                take(done + step * unroll + u)
            return carry

        spare = unroll - 1 if unroll == UNROLLS[-1] else 0
        steps = lax.div(count - done + spare, unroll)
        lax.fori_loop(0, steps, advance, 0)
        done = done + steps * unroll
    for out in outs:
        out[...] = accum[:chunk].astype(out.dtype)


def coarse_chunk(flip, listed, rights, lefts, dtypes, after=()):
    items, counts, a = listed
    held, width = rights[0].shape[0], a.shape[1]
    chunk = 3 * held * (held if flip is None else 1)
    n_left = lefts[0].shape[0] if flip is None else len(lefts)
    return pl.pallas_call(
        functools.partial(chunk_kernel, held, flip, len(lefts), len(dtypes)),
        out_shape=[jax.ShapeDtypeStruct((chunk, width, width), dtype) for dtype in dtypes],
        in_specs=[SMEM] * 2 + [VMEM] * (4 + len(lefts)) + [pl.BlockSpec(memory_space=pl.ANY)] * len(after),
        out_specs=[VMEM] * len(dtypes),
        scratch_shapes=[
            pltpu.VMEM((3 * held, width, width), jnp.bfloat16),
            pltpu.VMEM((n_left, width, width), jnp.bfloat16),
            pltpu.VMEM((chunk + 1, width, width), jnp.float32),
        ],
        compiler_params=pltpu.CompilerParams(vmem_limit_bytes=LIMIT),
        cost_estimate=pl.CostEstimate(flops=1 << 31, bytes_accessed=1 << 20, transcendentals=0),
        name="coarse_chunk",
    )(items, counts, a, *rights, *lefts, *after)


def add_kernel(n, *refs):
    xs, out = refs[:n], refs[-1]
    total = xs[0][...]
    for x in xs[1:]:
        total = total.astype(jnp.float32) + x[...].astype(jnp.float32)
    out[...] = total.astype(out.dtype)


def added(xs, dtype, after=()):
    return pl.pallas_call(
        functools.partial(add_kernel, len(xs)),
        out_shape=jax.ShapeDtypeStruct(xs[0].shape, dtype),
        in_specs=[VMEM] * len(xs) + [pl.BlockSpec(memory_space=pl.ANY)] * len(after),
        out_specs=VMEM,
        compiler_params=pltpu.CompilerParams(vmem_limit_bytes=LIMIT),
        name="added",
    )(*xs, *after)


def shifted(block, axis, distance):
    n = lax.axis_size(axis)
    return lax.ppermute(block, axis, [((i - distance) % n, i) for i in range(n)])


def line_of_four(a_tiles, a_row, a_col, a_count, p_tiles):
    me = lax.axis_index("col").reshape(1)
    held, width = p_tiles.shape[:2]
    stay = lambda x: pltpu.with_memory_space_constraint(x, pltpu.HBM)
    a_tiles, a_row, a_col, p_tiles = stay(a_tiles), stay(a_row), stay(a_col), stay(p_tiles)
    cross = lambda block, pairs: lax.ppermute(block, "col", pairs)
    flips = [[(i, i ^ m) for i in range(4)] for m in range(4)]
    far = {m: cross(p_tiles, flips[m]) for m in (2, 3, 1)}
    items, counts, a, own = plan(held, 4, me, a_row, a_col, a_count, a_tiles, p_tiles)
    below, above = shifted(own, "row", 1), shifted(own, "row", -1)
    keep = lambda x: pltpu.with_memory_space_constraint(x, pltpu.VMEM)
    listed = (items, counts, a)
    rights, lefts = [keep(below), own, keep(above)], [own] + [keep(far[m]) for m in (1, 2, 3)]

    bf16, f32 = jnp.bfloat16, jnp.float32
    (first,) = coarse_chunk(3, listed, rights, lefts, [bf16])
    got1 = cross(first, [(0, 1), (3, 2)])
    got3 = cross(added([first], bf16), [(1, 2), (2, 1)])
    second, wide = coarse_chunk(2, listed, rights, lefts, [bf16, f32], [first])
    got5 = cross(second, [(0, 2), (3, 1)])
    (third,) = coarse_chunk(1, listed, rights, lefts, [bf16], [second])
    got2 = cross(third, flips[1])
    joined = added([wide, got1], bf16, [third])
    got4 = cross(joined, [(1, 3), (2, 0)])
    (last,) = coarse_chunk(0, listed, rights, lefts, [f32], [joined])
    return added([last, got3, got5, got2, got4], bf16)


def any_columns(a_tiles, a_row, a_col, a_count, p_tiles):
    n = lax.axis_size("col")
    held = p_tiles.shape[0]
    total = 3 * held * held
    rights = [shifted(p_tiles, "row", 1), p_tiles, shifted(p_tiles, "row", -1)]
    row_side = lax.all_gather(p_tiles, "col", axis=0, tiled=True)
    me = jnp.zeros((1,), jnp.int32)
    items, counts, a, own = plan(held, 1, me, a_row, a_col, a_count, a_tiles, p_tiles)
    rights = (rights[0], own, rights[2])
    (sums,) = coarse_chunk(None, (items, counts, a), rights, [row_side], [jnp.bfloat16])
    parts = sums.reshape(n, total // n, *sums.shape[1:])
    parts = lax.all_to_all(parts, "col", 0, 0, tiled=True)
    return jnp.sum(parts.astype(jnp.float32), axis=0).astype(jnp.bfloat16)


def shards(a_tiles, a_row, a_col, a_count, p_tiles):
    special = lax.axis_size("col") == 4 and p_tiles.shape[0] == 4
    body = line_of_four if special else any_columns
    return body(a_tiles, a_row, a_col, a_count, p_tiles)


def solution(mesh):
    in_specs = (
        P(("row", "col"), None, None),
        P(("row", "col")),
        P(("row", "col")),
        P(("row", "col")),
        P(("row", "col"), None, None),
    )
    out_specs = P(("row", "col"), None, None)
    return jax.shard_map(shards, mesh=mesh, in_specs=in_specs, out_specs=out_specs, check_vma=False)
```

```python
import functools

import jax
import jax.numpy as jnp
from jax import lax
from jax.experimental import pallas as pl
from jax.experimental.pallas import tpu as pltpu
from jax.sharding import PartitionSpec as P

UNROLLS = (32, 16, 8, 4)
PARTS = ("twice", "once", "thrice", "below", "own", "above")
LIMIT = 12 * 1024 * 1024
VMEM = pl.BlockSpec(memory_space=pltpu.VMEM)
SMEM = pl.BlockSpec(memory_space=pltpu.SMEM)
HBM = pl.BlockSpec(memory_space=pltpu.HBM)


def bits(extent):
    return (extent - 1).bit_length()


def divide(x, n):
    if n & (n - 1):
        return lax.div(x, n), lax.rem(x, n)
    return x >> bits(n), x & (n - 1)


def plan_kernel(held, n, me, a_row, a_col, a_count, a, p, items, counts, a_out, p_out, sems):
    slots = a_row.shape[0]
    parts = sems.shape[0] - 1
    size = slots // parts
    copies = [pltpu.make_async_copy(p, p_out, sems.at[parts])]
    for i in range(parts):
        part = pl.ds(i * size, size)
        copies.append(pltpu.make_async_copy(a.at[part], a_out.at[part], sems.at[i]))
    for copy in copies:
        copy.start()
    field = 32 // n
    group = 8 if slots % 8 == 0 else 1
    live = a_count[0]

    def place(step, taken):
        for u in range(group):
            t = step * group + u
            row, col = a_row[t], a_col[t]
            d = divide(divide(row, held)[1] * n, held)[0]
            at = (taken >> (d * field)) & ((1 << min(field, 16)) - 1)
            items[d * slots + at] = t + (col << bits(slots)) + (row << (bits(slots) + bits(3 * held)))
            taken = taken + (jnp.where(t < live, 1, 0) << (d * field))
        return taken

    taken = lax.fori_loop(0, lax.div(live + group - 1, group), place, jnp.int32(0))
    for d in range(n):
        counts[d] = (taken >> (d * field)) & ((1 << min(field, 16)) - 1)
    counts[n] = me[0]
    for copy in copies:
        copy.wait()


def plan(held, n, me, a_row, a_col, a_count, a_tiles, p_tiles):
    return pl.pallas_call(
        functools.partial(plan_kernel, held, n),
        out_shape=(
            jax.ShapeDtypeStruct((n * a_row.shape[0],), jnp.int32),
            jax.ShapeDtypeStruct((n + 1,), jnp.int32),
            pltpu.VMEM(a_tiles.shape, a_tiles.dtype),
            pltpu.VMEM(p_tiles.shape, p_tiles.dtype),
        ),
        in_specs=[SMEM] * 4 + [HBM] * 2,
        out_specs=(SMEM, SMEM, VMEM, VMEM),
        scratch_shapes=[pltpu.SemaphoreType.DMA((5 if a_row.shape[0] % 4 == 0 else 2,))],
        compiler_params=pltpu.CompilerParams(vmem_limit_bytes=LIMIT),
        name="plan",
    )(me, a_row, a_col, a_count, a_tiles, p_tiles)


def chunk_kernel(held, flip, n_block, n_out, items, counts, a, *rest):
    blocks, outs, (right, left, accum) = rest[:n_block], rest[-3 - n_out : -3], rest[-3:]
    slots, chunk = a.shape[0], outs[0].shape[0]
    me = counts[counts.shape[0] - 1]
    d = 0 if flip is None else me ^ flip
    base, count = d * slots, counts[d]
    if flip is None:
        rights, rows = blocks[:3], blocks[3]
        for i in range(left.shape[0]):
            left[i] = rows[i].T
    else:
        part = dict(zip(PARTS, blocks))
        rights = part["below"], part["own"], part["above"]
        left[0] = part["own"][d].T
        left[1] = part["once"][d].T
        left[2] = part["twice"][d].T
        left[3] = part["thrice"][d].T
    for i, ref in enumerate(rights):
        right[i * held : (i + 1) * held] = ref[...]
    accum[...] = jnp.zeros_like(accum)

    def unpack(e):
        item = items[base + jnp.minimum(e, count - 1)]
        t, item = item & ((1 << bits(slots)) - 1), item >> bits(slots)
        col, row = item & ((1 << bits(3 * held)) - 1), item >> bits(3 * held)
        if flip is None:
            s = divide(row, held)[1] * (3 * held) + col
        else:
            row, s = divide(row, held)[0] ^ me, col
        return t, col, row, jnp.where(e < count, s, chunk)

    done = jnp.int32(0)
    for unroll, smaller in zip(UNROLLS, (*UNROLLS[1:], 0)):

        def advance(step, carry, done=done, unroll=unroll):
            work = [unpack(done + step * unroll + u) for u in range(unroll)]
            f32 = jnp.float32
            images = [jnp.dot(a[t], right[col], preferred_element_type=f32) for t, col, _, _ in work]
            images = [image.astype(jnp.bfloat16) for image in images]
            terms = [jnp.dot(left[w[2]], x, preferred_element_type=f32) for w, x in zip(work, images)]
            for w, term in zip(work, terms):
                accum[w[3]] += term
            return carry

        steps = lax.div(jnp.maximum(count - done, 0) + unroll - smaller - 1, unroll)
        lax.fori_loop(0, steps, advance, 0)
        done = done + steps * unroll
    for out in outs:
        out[...] = accum[:chunk].astype(out.dtype)


def coarse_chunk(flip, listed, blocks, dtypes, after=()):
    items, counts, a = listed
    held, width = blocks[0].shape[0], a.shape[1]
    chunk = 3 * held * (held if flip is None else 1)
    n_left = blocks[-1].shape[0] if flip is None else 4
    return pl.pallas_call(
        functools.partial(chunk_kernel, held, flip, len(blocks), len(dtypes)),
        out_shape=[jax.ShapeDtypeStruct((chunk, width, width), dtype) for dtype in dtypes],
        in_specs=[SMEM] * 2 + [VMEM] * (1 + len(blocks)) + [pl.BlockSpec(memory_space=pl.ANY)] * len(after),
        out_specs=[VMEM] * len(dtypes),
        scratch_shapes=[
            pltpu.VMEM((3 * held, width, width), jnp.bfloat16),
            pltpu.VMEM((n_left, width, width), jnp.bfloat16),
            pltpu.VMEM((chunk + 1, width, width), jnp.float32),
        ],
        compiler_params=pltpu.CompilerParams(vmem_limit_bytes=LIMIT),
        cost_estimate=pl.CostEstimate(flops=1 << 31, bytes_accessed=1 << 20, transcendentals=0),
        name="coarse_chunk",
    )(items, counts, a, *blocks, *after)


def add_kernel(n, *refs):
    xs, out = refs[:n], refs[-1]
    total = xs[0][...]
    for x in xs[1:]:
        total = total.astype(jnp.float32) + x[...].astype(jnp.float32)
    out[...] = total.astype(out.dtype)


def added(xs, dtype, after=()):
    return pl.pallas_call(
        functools.partial(add_kernel, len(xs)),
        out_shape=jax.ShapeDtypeStruct(xs[0].shape, dtype),
        in_specs=[VMEM] * len(xs) + [pl.BlockSpec(memory_space=pl.ANY)] * len(after),
        out_specs=VMEM,
        compiler_params=pltpu.CompilerParams(vmem_limit_bytes=LIMIT),
        name="added",
    )(*xs, *after)


def shifted(block, axis, distance):
    n = lax.axis_size(axis)
    return lax.ppermute(block, axis, [((i - distance) % n, i) for i in range(n)])


def line_of_four(a_tiles, a_row, a_col, a_count, p_tiles):
    me = lax.axis_index("col").reshape(1)
    held, width = p_tiles.shape[:2]
    stay = lambda x: pltpu.with_memory_space_constraint(x, pltpu.HBM)
    a_tiles, a_row, a_col, p_tiles = stay(a_tiles), stay(a_row), stay(a_col), stay(p_tiles)
    cross = lambda block, pairs: lax.ppermute(block, "col", pairs)
    flips = [[(i, i ^ m) for i in range(4)] for m in range(4)]
    once, twice, thrice = (cross(p_tiles, flips[m]) for m in (1, 2, 3))
    items, counts, a, own = plan(held, 4, me, a_row, a_col, a_count, a_tiles, p_tiles)
    below, above = shifted(p_tiles, "row", 1), shifted(p_tiles, "row", -1)
    part = dict(once=once, twice=twice, thrice=thrice, below=below, above=above)
    part = {name: pltpu.with_memory_space_constraint(x, pltpu.VMEM) for name, x in part.items()}
    part["own"] = own
    listed, blocks = (items, counts, a), [part[name] for name in PARTS]

    bf16, f32 = jnp.bfloat16, jnp.float32
    (first,) = coarse_chunk(3, listed, blocks, [bf16])
    got1 = cross(first, [(0, 1), (3, 2)])
    got3 = cross(added([first], bf16), [(1, 2), (2, 1)])
    second, wide = coarse_chunk(2, listed, blocks, [bf16, f32], [first])
    got5 = cross(second, [(0, 2), (3, 1)])
    (third,) = coarse_chunk(1, listed, blocks, [bf16], [second])
    got2 = cross(third, flips[1])
    joined = added([wide, got1], bf16, [third])
    got4 = cross(joined, [(1, 3), (2, 0)])
    (last,) = coarse_chunk(0, listed, blocks, [f32], [joined])
    most = added([last, got3, got5, got2], f32)
    return added([most, got4], bf16)


def any_columns(a_tiles, a_row, a_col, a_count, p_tiles):
    n = lax.axis_size("col")
    held = p_tiles.shape[0]
    total = 3 * held * held
    rights = [shifted(p_tiles, "row", 1), p_tiles, shifted(p_tiles, "row", -1)]
    row_side = lax.all_gather(p_tiles, "col", axis=0, tiled=True)
    me = jnp.zeros((1,), jnp.int32)
    items, counts, a, own = plan(held, 1, me, a_row, a_col, a_count, a_tiles, p_tiles)
    blocks = (rights[0], own, rights[2], row_side)
    (sums,) = coarse_chunk(None, (items, counts, a), blocks, [jnp.bfloat16])
    parts = sums.reshape(n, total // n, *sums.shape[1:])
    parts = lax.all_to_all(parts, "col", 0, 0, tiled=True)
    return jnp.sum(parts.astype(jnp.float32), axis=0).astype(jnp.bfloat16)


def shards(a_tiles, a_row, a_col, a_count, p_tiles):
    special = lax.axis_size("col") == 4 and p_tiles.shape[0] == 4
    body = line_of_four if special else any_columns
    return body(a_tiles, a_row, a_col, a_count, p_tiles)


def solution(mesh):
    in_specs = (
        P(("row", "col"), None, None),
        P(("row", "col")),
        P(("row", "col")),
        P(("row", "col")),
        P(("row", "col"), None, None),
    )
    out_specs = P(("row", "col"), None, None)
    return jax.shard_map(shards, mesh=mesh, in_specs=in_specs, out_specs=out_specs, check_vma=False)
```

```python
import functools

import jax
import jax.numpy as jnp
from jax import lax
from jax.experimental import pallas as pl
from jax.experimental.pallas import tpu as pltpu
from jax.sharding import PartitionSpec as P

UNROLLS = (32, 16, 8, 4)
PARTS = ("twice", "once", "thrice", "below", "own", "above")
LIMIT = 12 * 1024 * 1024
VMEM = pl.BlockSpec(memory_space=pltpu.VMEM)
SMEM = pl.BlockSpec(memory_space=pltpu.SMEM)
HBM = pl.BlockSpec(memory_space=pltpu.HBM)


def bits(extent):
    return (extent - 1).bit_length()


def divide(x, n):
    if n & (n - 1):
        return lax.div(x, n), lax.rem(x, n)
    return x >> bits(n), x & (n - 1)


def plan_kernel(held, n, me, a_row, a_col, a_count, a, p, items, counts, a_out, p_out, sems):
    slots = a_row.shape[0]
    parts = sems.shape[0] - 1
    size = slots // parts
    copies = [pltpu.make_async_copy(p, p_out, sems.at[parts])]
    for i in range(parts):
        part = pl.ds(i * size, size)
        copies.append(pltpu.make_async_copy(a.at[part], a_out.at[part], sems.at[i]))
    for copy in copies:
        copy.start()
    field = 32 // n
    group = 8 if slots % 8 == 0 else 1
    live = a_count[0]

    def place(step, taken):
        for u in range(group):
            t = step * group + u
            row, col = a_row[t], a_col[t]
            d = divide(divide(row, held)[1] * n, held)[0]
            at = (taken >> (d * field)) & ((1 << min(field, 16)) - 1)
            items[d * slots + at] = t + (col << bits(slots)) + (row << (bits(slots) + bits(3 * held)))
            taken = taken + (jnp.where(t < live, 1, 0) << (d * field))
        return taken

    taken = lax.fori_loop(0, lax.div(live + group - 1, group), place, jnp.int32(0))
    for d in range(n):
        counts[d] = (taken >> (d * field)) & ((1 << min(field, 16)) - 1)
    counts[n] = me[0]
    for copy in copies:
        copy.wait()


def plan(held, n, me, a_row, a_col, a_count, a_tiles, p_tiles):
    return pl.pallas_call(
        functools.partial(plan_kernel, held, n),
        out_shape=(
            pltpu.SMEM((n * a_row.shape[0],), jnp.int32),
            pltpu.SMEM((n + 1,), jnp.int32),
            pltpu.VMEM(a_tiles.shape, a_tiles.dtype),
            pltpu.VMEM(p_tiles.shape, p_tiles.dtype),
        ),
        in_specs=[SMEM] * 4 + [HBM] * 2,
        out_specs=(SMEM, SMEM, VMEM, VMEM),
        scratch_shapes=[pltpu.SemaphoreType.DMA((5 if a_row.shape[0] % 4 == 0 else 2,))],
        compiler_params=pltpu.CompilerParams(vmem_limit_bytes=LIMIT),
        name="plan",
    )(me, a_row, a_col, a_count, a_tiles, p_tiles)


def chunk_kernel(held, pick, n_block, parts, items, counts, a, *rest):
    blocks, outs, (right, left, accum) = rest[:n_block], rest[-3 - len(parts) : -3], rest[-3:]
    slots, chunk = a.shape[0], accum.shape[0] - 1
    me = counts[counts.shape[0] - 1]
    d = 0 if pick is None else sum(jnp.where(me == i, x, 0) for i, x in enumerate(pick))
    base, count = d * slots, counts[d]
    if pick is None:
        rights, rows = blocks[:3], blocks[3]
        for i in range(left.shape[0]):
            left[i] = rows[i].T
    else:
        part = dict(zip(PARTS, blocks))
        rights = part["below"], part["own"], part["above"]
        left[0] = part["own"][d].T
        left[1] = part["once"][d].T
        left[2] = part["twice"][d].T
        left[3] = part["thrice"][d].T
    for i, ref in enumerate(rights):
        right[i * held : (i + 1) * held] = ref[...]
    accum[...] = jnp.zeros_like(accum)

    def unpack(e):
        item = items[base + jnp.minimum(e, count - 1)]
        t, item = item & ((1 << bits(slots)) - 1), item >> bits(slots)
        col, row = item & ((1 << bits(3 * held)) - 1), item >> bits(3 * held)
        if pick is None:
            s = divide(row, held)[1] * (3 * held) + col
        else:
            row, s = divide(row, held)[0] ^ me, col
        return t, col, row, jnp.where(e < count, s, chunk)

    done = jnp.int32(0)
    for unroll, smaller in zip(UNROLLS, (*UNROLLS[1:], 0)):

        def advance(step, carry, done=done, unroll=unroll):
            work = [unpack(done + step * unroll + u) for u in range(unroll)]
            f32 = jnp.float32
            images = [jnp.dot(a[t], right[col], preferred_element_type=f32) for t, col, _, _ in work]
            images = [image.astype(jnp.bfloat16) for image in images]
            terms = [jnp.dot(left[w[2]], x, preferred_element_type=f32) for w, x in zip(work, images)]
            for w, term in zip(work, terms):
                accum[w[3]] += term
            return carry

        steps = lax.div(jnp.maximum(count - done, 0) + unroll - smaller - 1, unroll)
        lax.fori_loop(0, steps, advance, 0)
        done = done + steps * unroll
    for out, start in zip(outs, parts):
        out[...] = accum[start : start + out.shape[0]].astype(out.dtype)


def coarse_chunk(pick, listed, blocks, outs, after=()):
    items, counts, a = listed
    held, width = blocks[0].shape[0], a.shape[1]
    chunk = 3 * held * (held if pick is None else 1)
    n_left = blocks[-1].shape[0] if pick is None else 4
    return pl.pallas_call(
        functools.partial(chunk_kernel, held, pick, len(blocks), [start for start, _, _ in outs]),
        out_shape=[jax.ShapeDtypeStruct((end - start, width, width), dtype) for start, end, dtype in outs],
        in_specs=[SMEM] * 2 + [VMEM] * (1 + len(blocks)) + [pl.BlockSpec(memory_space=pl.ANY)] * len(after),
        out_specs=[VMEM] * len(outs),
        scratch_shapes=[
            pltpu.VMEM((3 * held, width, width), jnp.bfloat16),
            pltpu.VMEM((n_left, width, width), jnp.bfloat16),
            pltpu.VMEM((chunk + 1, width, width), jnp.float32),
        ],
        compiler_params=pltpu.CompilerParams(vmem_limit_bytes=LIMIT),
        cost_estimate=pl.CostEstimate(flops=1 << 31, bytes_accessed=1 << 20, transcendentals=0),
        name="coarse_chunk",
    )(items, counts, a, *blocks, *after)


def mix_kernel(counts, x, y, z, *rest):
    out = rest[-1]
    me = counts[counts.shape[0] - 1]
    f32 = jnp.float32
    total = y[...].astype(f32) + z[...].astype(f32)
    out[...] = jnp.where((me == 0) | (me == 3), x[...].astype(f32), total).astype(out.dtype)


def mixed(counts, x, y, z, after=()):
    return pl.pallas_call(
        mix_kernel,
        out_shape=jax.ShapeDtypeStruct(x.shape, x.dtype),
        in_specs=[SMEM] + [VMEM] * 3 + [pl.BlockSpec(memory_space=pl.ANY)] * len(after),
        out_specs=VMEM,
        compiler_params=pltpu.CompilerParams(vmem_limit_bytes=LIMIT),
        name="mixed",
    )(counts, x, y, z, *after)


def finish_kernel(counts, most, far_a, far_b, near_a, near_b, out):
    me = counts[counts.shape[0] - 1]
    half = far_a.shape[0]
    f32 = jnp.float32
    end = (me == 0) | (me == 3)
    for i, (far, near) in enumerate(((far_a, near_a), (far_b, near_b))):
        part = slice(i * half, (i + 1) * half)
        out[part] = (most[part] + jnp.where(end, far[...], near[...]).astype(f32)).astype(out.dtype)


def finished(counts, most, *got):
    return pl.pallas_call(
        finish_kernel,
        out_shape=jax.ShapeDtypeStruct(most.shape, got[0].dtype),
        in_specs=[SMEM] + [VMEM] * 5,
        out_specs=VMEM,
        compiler_params=pltpu.CompilerParams(vmem_limit_bytes=LIMIT),
        name="finished",
    )(counts, most, *got)


def add_kernel(n, *refs):
    xs, out = refs[:n], refs[-1]
    total = xs[0][...]
    for x in xs[1:]:
        total = total.astype(jnp.float32) + x[...].astype(jnp.float32)
    out[...] = total.astype(out.dtype)


def added(xs, dtype, after=()):
    return pl.pallas_call(
        functools.partial(add_kernel, len(xs)),
        out_shape=jax.ShapeDtypeStruct(xs[0].shape, dtype),
        in_specs=[VMEM] * len(xs) + [pl.BlockSpec(memory_space=pl.ANY)] * len(after),
        out_specs=VMEM,
        compiler_params=pltpu.CompilerParams(vmem_limit_bytes=LIMIT),
        name="added",
    )(*xs, *after)


def shifted(block, axis, distance):
    n = lax.axis_size(axis)
    return lax.ppermute(block, axis, [((i - distance) % n, i) for i in range(n)])


def line_of_four(a_tiles, a_row, a_col, a_count, p_tiles):
    me = lax.axis_index("col").reshape(1)
    held, width = p_tiles.shape[:2]
    stay = lambda x: pltpu.with_memory_space_constraint(x, pltpu.HBM)
    a_tiles, a_row, a_col, p_tiles = stay(a_tiles), stay(a_row), stay(a_col), stay(p_tiles)
    cross = lambda block, pairs: lax.ppermute(block, "col", pairs)
    flips = [[(i, i ^ m) for i in range(4)] for m in range(4)]
    once, twice, thrice = (cross(p_tiles, flips[m]) for m in (1, 2, 3))
    items, counts, a, own = plan(held, 4, me, a_row, a_col, a_count, a_tiles, p_tiles)
    below, above = shifted(p_tiles, "row", 1), shifted(p_tiles, "row", -1)
    part = dict(once=once, twice=twice, thrice=thrice, below=below, above=above)
    part = {name: pltpu.with_memory_space_constraint(x, pltpu.VMEM) for name, x in part.items()}
    part["own"] = own
    listed, blocks = (items, counts, a), [part[name] for name in PARTS]

    bf16, f32 = jnp.bfloat16, jnp.float32
    chunk, half = 3 * held, 3 * held // 2
    cut = [(0, half), (half, chunk)]
    halves = [(*c, bf16) for c in cut] + [(*c, f32) for c in cut]
    ends, middles, over = [(0, 1), (3, 2)], [(1, 2), (2, 1)], [(1, 3), (2, 0)]
    *first, wide_a, wide_b = coarse_chunk((3, 3, 0, 0), listed, blocks, halves)
    got1 = cross(first[0], ends)
    *second, next_a, next_b = coarse_chunk((2, 2, 1, 1), listed, blocks, halves, first[:1])
    got2 = cross(added(first[1:], bf16, second[:1]), ends)
    sent3 = mixed(counts, second[0], wide_a, got1)
    got3 = cross(sent3, ends + over)
    sent4 = mixed(counts, second[1], wide_b, got2, [sent3])
    got4 = cross(sent4, ends + over)
    (third,) = coarse_chunk((1, 0, 3, 2), listed, blocks, [(0, chunk, bf16)], [sent4])
    got5 = cross(third, flips[1])
    sent6 = added([next_a, got3], bf16, [third])
    got6 = cross(sent6, middles)
    sent7 = added([next_b, got4], bf16, [sent6])
    got7 = cross(sent7, middles)
    (last,) = coarse_chunk((0, 1, 2, 3), listed, blocks, [(0, chunk, f32)], [sent7])
    return finished(counts, added([last, got5], f32), got3, got4, got6, got7)


def any_columns(a_tiles, a_row, a_col, a_count, p_tiles):
    n = lax.axis_size("col")
    held = p_tiles.shape[0]
    total = 3 * held * held
    rights = [shifted(p_tiles, "row", 1), p_tiles, shifted(p_tiles, "row", -1)]
    row_side = lax.all_gather(p_tiles, "col", axis=0, tiled=True)
    me = jnp.zeros((1,), jnp.int32)
    items, counts, a, own = plan(held, 1, me, a_row, a_col, a_count, a_tiles, p_tiles)
    blocks = (rights[0], own, rights[2], row_side)
    (sums,) = coarse_chunk(None, (items, counts, a), blocks, [(0, total, jnp.bfloat16)])
    parts = sums.reshape(n, total // n, *sums.shape[1:])
    parts = lax.all_to_all(parts, "col", 0, 0, tiled=True)
    return jnp.sum(parts.astype(jnp.float32), axis=0).astype(jnp.bfloat16)


def shards(a_tiles, a_row, a_col, a_count, p_tiles):
    special = lax.axis_size("col") == 4 and p_tiles.shape[0] == 4
    body = line_of_four if special else any_columns
    return body(a_tiles, a_row, a_col, a_count, p_tiles)


def solution(mesh):
    in_specs = (
        P(("row", "col"), None, None),
        P(("row", "col")),
        P(("row", "col")),
        P(("row", "col")),
        P(("row", "col"), None, None),
    )
    out_specs = P(("row", "col"), None, None)
    return jax.shard_map(shards, mesh=mesh, in_specs=in_specs, out_specs=out_specs, check_vma=False)
```

```python
import functools

import jax
import jax.numpy as jnp
from jax import lax
from jax.experimental import pallas as pl
from jax.experimental.pallas import tpu as pltpu
from jax.sharding import PartitionSpec as P

UNROLLS = (32, 16, 8, 4)
PARTS = ("twice", "once", "thrice", "below", "own", "above")
LIMIT = 12 * 1024 * 1024
VMEM = pl.BlockSpec(memory_space=pltpu.VMEM)
SMEM = pl.BlockSpec(memory_space=pltpu.SMEM)
HBM = pl.BlockSpec(memory_space=pltpu.HBM)


def bits(extent):
    return (extent - 1).bit_length()


def divide(x, n):
    if n & (n - 1):
        return lax.div(x, n), lax.rem(x, n)
    return x >> bits(n), x & (n - 1)


def plan_kernel(held, n, me, a_row, a_col, a_count, a, p, items, counts, a_out, p_out, sems):
    slots = a_row.shape[0]
    parts = sems.shape[0] - 1
    size = slots // parts
    copies = [pltpu.make_async_copy(p, p_out, sems.at[parts])]
    for i in range(parts):
        part = pl.ds(i * size, size)
        copies.append(pltpu.make_async_copy(a.at[part], a_out.at[part], sems.at[i]))
    for copy in copies:
        copy.start()
    field = 32 // n
    group = 8 if slots % 8 == 0 else 1
    live = a_count[0]

    def place(step, taken):
        for u in range(group):
            t = step * group + u
            row, col = a_row[t], a_col[t]
            d = divide(divide(row, held)[1] * n, held)[0]
            at = (taken >> (d * field)) & ((1 << min(field, 16)) - 1)
            items[d * slots + at] = t + (col << bits(slots)) + (row << (bits(slots) + bits(3 * held)))
            taken = taken + (jnp.where(t < live, 1, 0) << (d * field))
        return taken

    taken = lax.fori_loop(0, lax.div(live + group - 1, group), place, jnp.int32(0))
    for d in range(n):
        counts[d] = (taken >> (d * field)) & ((1 << min(field, 16)) - 1)
    counts[n] = me[0]
    for copy in copies:
        copy.wait()


def plan(held, n, me, a_row, a_col, a_count, a_tiles, p_tiles):
    return pl.pallas_call(
        functools.partial(plan_kernel, held, n),
        out_shape=(
            pltpu.SMEM((n * a_row.shape[0],), jnp.int32),
            pltpu.SMEM((n + 1,), jnp.int32),
            pltpu.VMEM(a_tiles.shape, a_tiles.dtype),
            pltpu.VMEM(p_tiles.shape, p_tiles.dtype),
        ),
        in_specs=[SMEM] * 4 + [HBM] * 2,
        out_specs=(SMEM, SMEM, VMEM, VMEM),
        scratch_shapes=[pltpu.SemaphoreType.DMA((5 if a_row.shape[0] % 4 == 0 else 2,))],
        compiler_params=pltpu.CompilerParams(vmem_limit_bytes=LIMIT),
        name="plan",
    )(me, a_row, a_col, a_count, a_tiles, p_tiles)


def chunk_kernel(held, pick, n_block, parts, items, counts, a, *rest):
    blocks, outs, (right, left, accum) = rest[:n_block], rest[-3 - len(parts) : -3], rest[-3:]
    slots, chunk = a.shape[0], accum.shape[0] - 1
    me = counts[counts.shape[0] - 1]
    d = 0 if pick is None else sum(jnp.where(me == i, x, 0) for i, x in enumerate(pick))

    @pl.when(d >= 0)
    def _():
        base, count = d * slots, counts[d]
        if pick is None:
            rights, rows = blocks[:3], blocks[3]
            for i in range(left.shape[0]):
                left[i] = rows[i].T
        else:
            part = dict(zip(PARTS, blocks))
            rights = part["below"], part["own"], part["above"]
            left[0] = part["own"][d].T
            left[1] = part["once"][d].T
            left[2] = part["twice"][d].T
            left[3] = part["thrice"][d].T
        for i, ref in enumerate(rights):
            right[i * held : (i + 1) * held] = ref[...]
        accum[...] = jnp.zeros_like(accum)

        def unpack(e):
            item = items[base + jnp.minimum(e, count - 1)]
            t, item = item & ((1 << bits(slots)) - 1), item >> bits(slots)
            col, row = item & ((1 << bits(3 * held)) - 1), item >> bits(3 * held)
            if pick is None:
                s = divide(row, held)[1] * (3 * held) + col
            else:
                row, s = divide(row, held)[0] ^ me, col
            return t, col, row, jnp.where(e < count, s, chunk)

        done = jnp.int32(0)
        for unroll, smaller in zip(UNROLLS, (*UNROLLS[1:], 0)):

            def advance(step, carry, done=done, unroll=unroll):
                work = [unpack(done + step * unroll + u) for u in range(unroll)]
                f32 = jnp.float32
                images = [jnp.dot(a[t], right[col], preferred_element_type=f32) for t, col, _, _ in work]
                images = [image.astype(jnp.bfloat16) for image in images]
                terms = [jnp.dot(left[w[2]], x, preferred_element_type=f32) for w, x in zip(work, images)]
                for w, term in zip(work, terms):
                    accum[w[3]] += term
                return carry

            steps = lax.div(jnp.maximum(count - done, 0) + unroll - smaller - 1, unroll)
            lax.fori_loop(0, steps, advance, 0)
            done = done + steps * unroll
        for out, start in zip(outs, parts):
            out[...] = accum[start : start + out.shape[0]].astype(out.dtype)


def coarse_chunk(pick, listed, blocks, outs, after=()):
    items, counts, a = listed
    held, width = blocks[0].shape[0], a.shape[1]
    chunk = 3 * held * (held if pick is None else 1)
    n_left = blocks[-1].shape[0] if pick is None else 4
    return pl.pallas_call(
        functools.partial(chunk_kernel, held, pick, len(blocks), [start for start, _, _ in outs]),
        out_shape=[jax.ShapeDtypeStruct((end - start, width, width), dtype) for start, end, dtype in outs],
        in_specs=[SMEM] * 2 + [VMEM] * (1 + len(blocks)) + [pl.BlockSpec(memory_space=pl.ANY)] * len(after),
        out_specs=[VMEM] * len(outs),
        scratch_shapes=[
            pltpu.VMEM((3 * held, width, width), jnp.bfloat16),
            pltpu.VMEM((n_left, width, width), jnp.bfloat16),
            pltpu.VMEM((chunk + 1, width, width), jnp.float32),
        ],
        compiler_params=pltpu.CompilerParams(vmem_limit_bytes=LIMIT),
        cost_estimate=pl.CostEstimate(flops=1 << 31, bytes_accessed=1 << 20, transcendentals=0),
        name="coarse_chunk",
    )(items, counts, a, *blocks, *after)


def mix_kernel(counts, x, y, z, *rest):
    out = rest[-1]
    me = counts[counts.shape[0] - 1]
    f32 = jnp.float32
    total = y[...].astype(f32) + z[...].astype(f32)
    out[...] = jnp.where((me == 0) | (me == 3), x[...].astype(f32), total).astype(out.dtype)


def mixed(counts, x, y, z, after=()):
    return pl.pallas_call(
        mix_kernel,
        out_shape=jax.ShapeDtypeStruct(x.shape, x.dtype),
        in_specs=[SMEM] + [VMEM] * 3 + [pl.BlockSpec(memory_space=pl.ANY)] * len(after),
        out_specs=VMEM,
        compiler_params=pltpu.CompilerParams(vmem_limit_bytes=LIMIT),
        name="mixed",
    )(counts, x, y, z, *after)


def most_kernel(counts, at_end, elsewhere, far, near, out):
    me = counts[counts.shape[0] - 1]
    end = (me == 0) | (me == 3)
    f32 = jnp.float32
    out[...] = jnp.where(end, at_end[...], elsewhere[...]) + jnp.where(end, far[...], near[...]).astype(f32)


def finish_kernel(most_a, most_b, got, out):
    half = most_a.shape[0]
    for i, most in enumerate((most_a, most_b)):
        part = slice(i * half, (i + 1) * half)
        out[part] = (most[...] + got[part].astype(jnp.float32)).astype(out.dtype)


def finished(counts, own, got, last):
    params = pltpu.CompilerParams(vmem_limit_bytes=LIMIT)
    most = [
        pl.pallas_call(
            most_kernel,
            out_shape=jax.ShapeDtypeStruct(x.shape, x.dtype),
            in_specs=[SMEM] + [VMEM] * 4,
            out_specs=VMEM,
            compiler_params=params,
            name="most",
        )(counts, x, y, far, near)
        for x, y, far, near in zip(*own, *got)
    ]
    return pl.pallas_call(
        finish_kernel,
        out_shape=jax.ShapeDtypeStruct(last.shape, last.dtype),
        in_specs=[VMEM] * 3,
        out_specs=VMEM,
        compiler_params=params,
        name="finished",
    )(*most, last)


def add_kernel(n, *refs):
    xs, out = refs[:n], refs[-1]
    total = xs[0][...]
    for x in xs[1:]:
        total = total.astype(jnp.float32) + x[...].astype(jnp.float32)
    out[...] = total.astype(out.dtype)


def added(xs, dtype, after=()):
    return pl.pallas_call(
        functools.partial(add_kernel, len(xs)),
        out_shape=jax.ShapeDtypeStruct(xs[0].shape, dtype),
        in_specs=[VMEM] * len(xs) + [pl.BlockSpec(memory_space=pl.ANY)] * len(after),
        out_specs=VMEM,
        compiler_params=pltpu.CompilerParams(vmem_limit_bytes=LIMIT),
        name="added",
    )(*xs, *after)


def shifted(block, axis, distance):
    n = lax.axis_size(axis)
    return lax.ppermute(block, axis, [((i - distance) % n, i) for i in range(n)])


def line_of_four(a_tiles, a_row, a_col, a_count, p_tiles):
    me = lax.axis_index("col").reshape(1)
    held, width = p_tiles.shape[:2]
    stay = lambda x: pltpu.with_memory_space_constraint(x, pltpu.HBM)
    a_tiles, a_row, a_col, p_tiles = stay(a_tiles), stay(a_row), stay(a_col), stay(p_tiles)
    cross = lambda block, pairs: lax.ppermute(block, "col", pairs)
    flips = [[(i, i ^ m) for i in range(4)] for m in range(4)]
    once, twice, thrice = (cross(p_tiles, flips[m]) for m in (1, 2, 3))
    items, counts, a, own = plan(held, 4, me, a_row, a_col, a_count, a_tiles, p_tiles)
    below, above = shifted(p_tiles, "row", 1), shifted(p_tiles, "row", -1)
    part = dict(once=once, twice=twice, thrice=thrice, below=below, above=above)
    part = {name: pltpu.with_memory_space_constraint(x, pltpu.VMEM) for name, x in part.items()}
    part["own"] = own
    listed, blocks = (items, counts, a), [part[name] for name in PARTS]

    bf16, f32 = jnp.bfloat16, jnp.float32
    chunk, half = 3 * held, 3 * held // 2
    cut = [(0, half), (half, chunk)]
    narrow, full = [(*c, bf16) for c in cut], [(*c, f32) for c in cut]
    ends, middles, over = [(0, 1), (3, 2)], [(1, 2), (2, 1)], [(1, 3), (2, 0)]
    part = lambda pick, outs, after=(): coarse_chunk(pick, listed, blocks, outs, after)
    first = part((3, -1, -1, 0), narrow)
    got1 = cross(first[0], ends)
    *second, wide_a, wide_b = part((2, 3, 0, 1), narrow + full, first[:1])
    got2 = cross(added(first[1:], bf16, second[:1]), ends)
    sent3 = mixed(counts, second[0], wide_a, got1)
    got3 = cross(sent3, ends + over)
    sent4 = mixed(counts, second[1], wide_b, got2, [sent3])
    got4 = cross(sent4, ends + over)
    (third,) = part((1, 0, 3, 2), [(0, chunk, bf16)], [sent4])
    got5 = cross(third, flips[1])
    fourth = part((0, 2, 1, 3), full, [third])
    sent6 = added([fourth[0], got3], bf16, [third])
    got6 = cross(sent6, middles)
    sent7 = added([fourth[1], got4], bf16, [sent6])
    got7 = cross(sent7, middles)
    fifth = part((-1, 1, 2, -1), full, [sent7])
    return finished(counts, [fourth, fifth], [(got3, got4), (got6, got7)], got5)


def any_columns(a_tiles, a_row, a_col, a_count, p_tiles):
    n = lax.axis_size("col")
    held = p_tiles.shape[0]
    total = 3 * held * held
    rights = [shifted(p_tiles, "row", 1), p_tiles, shifted(p_tiles, "row", -1)]
    row_side = lax.all_gather(p_tiles, "col", axis=0, tiled=True)
    me = jnp.zeros((1,), jnp.int32)
    items, counts, a, own = plan(held, 1, me, a_row, a_col, a_count, a_tiles, p_tiles)
    blocks = (rights[0], own, rights[2], row_side)
    (sums,) = coarse_chunk(None, (items, counts, a), blocks, [(0, total, jnp.bfloat16)])
    parts = sums.reshape(n, total // n, *sums.shape[1:])
    parts = lax.all_to_all(parts, "col", 0, 0, tiled=True)
    return jnp.sum(parts.astype(jnp.float32), axis=0).astype(jnp.bfloat16)


def shards(a_tiles, a_row, a_col, a_count, p_tiles):
    special = lax.axis_size("col") == 4 and p_tiles.shape[0] == 4
    body = line_of_four if special else any_columns
    return body(a_tiles, a_row, a_col, a_count, p_tiles)


def solution(mesh):
    in_specs = (
        P(("row", "col"), None, None),
        P(("row", "col")),
        P(("row", "col")),
        P(("row", "col")),
        P(("row", "col"), None, None),
    )
    out_specs = P(("row", "col"), None, None)
    return jax.shard_map(shards, mesh=mesh, in_specs=in_specs, out_specs=out_specs, check_vma=False)
```

```python
import functools

import jax
import jax.numpy as jnp
from jax import lax
from jax.experimental import pallas as pl
from jax.experimental.pallas import tpu as pltpu
from jax.sharding import PartitionSpec as P

UNROLLS = (32, 16, 8, 4)
PARTS = ("opposite", "across", "beside", "below", "own", "above")
LIMIT = 12 * 1024 * 1024
VMEM = pl.BlockSpec(memory_space=pltpu.VMEM)
SMEM = pl.BlockSpec(memory_space=pltpu.SMEM)
HBM = pl.BlockSpec(memory_space=pltpu.HBM)


def bits(extent):
    return (extent - 1).bit_length()


def divide(x, n):
    if n & (n - 1):
        return lax.div(x, n), lax.rem(x, n)
    return x >> bits(n), x & (n - 1)


def plan_kernel(held, n, me, a_row, a_col, a_count, a, p, items, counts, a_out, p_out, sems):
    slots = a_row.shape[0]
    parts = sems.shape[0] - 1
    size = slots // parts
    copies = [pltpu.make_async_copy(p, p_out, sems.at[parts])]
    for i in range(parts):
        part = pl.ds(i * size, size)
        copies.append(pltpu.make_async_copy(a.at[part], a_out.at[part], sems.at[i]))
    for copy in copies:
        copy.start()
    field = 32 // n
    group = 8 if slots % 8 == 0 else 1
    live = a_count[0]

    def place(step, taken):
        for u in range(group):
            t = step * group + u
            row, col = a_row[t], a_col[t]
            d = divide(divide(row, held)[1] * n, held)[0]
            at = (taken >> (d * field)) & ((1 << min(field, 16)) - 1)
            items[d * slots + at] = t + (col << bits(slots)) + (row << (bits(slots) + bits(3 * held)))
            taken = taken + (jnp.where(t < live, 1, 0) << (d * field))
        return taken

    taken = lax.fori_loop(0, lax.div(live + group - 1, group), place, jnp.int32(0))
    for d in range(n):
        counts[d] = (taken >> (d * field)) & ((1 << min(field, 16)) - 1)
    counts[n] = me[0]
    for copy in copies:
        copy.wait()


def plan(held, n, me, a_row, a_col, a_count, a_tiles, p_tiles):
    return pl.pallas_call(
        functools.partial(plan_kernel, held, n),
        out_shape=(
            pltpu.SMEM((n * a_row.shape[0],), jnp.int32),
            pltpu.SMEM((n + 1,), jnp.int32),
            pltpu.VMEM(a_tiles.shape, a_tiles.dtype),
            pltpu.VMEM(p_tiles.shape, p_tiles.dtype),
        ),
        in_specs=[SMEM] * 4 + [HBM] * 2,
        out_specs=(SMEM, SMEM, VMEM, VMEM),
        scratch_shapes=[pltpu.SemaphoreType.DMA((5 if a_row.shape[0] % 4 == 0 else 2,))],
        compiler_params=pltpu.CompilerParams(vmem_limit_bytes=LIMIT),
        name="plan",
    )(me, a_row, a_col, a_count, a_tiles, p_tiles)


def chunk_kernel(held, pick, n_block, parts, items, counts, a, *rest):
    blocks, outs, (right, left, accum) = rest[:n_block], rest[-3 - len(parts) : -3], rest[-3:]
    slots, chunk = a.shape[0], accum.shape[0] - 1
    me = counts[counts.shape[0] - 1]
    d = 0 if pick is None else sum(jnp.where(me == i, x, 0) for i, x in enumerate(pick))

    @pl.when(d >= 0)
    def _():
        base, count = d * slots, counts[d]
        if pick is None:
            rights, rows = blocks[:3], blocks[3]
            for i in range(left.shape[0]):
                left[i] = rows[i].T
        else:
            part = dict(zip(PARTS, blocks))
            rights = part["below"], part["own"], part["above"]
            left[0] = part["own"][d].T
            end = (me == 0) | (me == 3)
            left[1] = jnp.where(end, part["beside"][d], part["across"][d]).T
            left[2] = jnp.where(end, part["across"][d], part["beside"][d]).T
            left[3] = part["opposite"][d].T
        for i, ref in enumerate(rights):
            right[i * held : (i + 1) * held] = ref[...]
        accum[...] = jnp.zeros_like(accum)

        def unpack(e):
            item = items[base + jnp.minimum(e, count - 1)]
            t, item = item & ((1 << bits(slots)) - 1), item >> bits(slots)
            col, row = item & ((1 << bits(3 * held)) - 1), item >> bits(3 * held)
            if pick is None:
                s = divide(row, held)[1] * (3 * held) + col
            else:
                row, s = divide(row, held)[0] ^ me, col
            return t, col, row, jnp.where(e < count, s, chunk)

        done = jnp.int32(0)
        for unroll, smaller in zip(UNROLLS, (*UNROLLS[1:], 0)):

            def advance(step, carry, done=done, unroll=unroll):
                work = [unpack(done + step * unroll + u) for u in range(unroll)]
                f32 = jnp.float32
                images = [jnp.dot(a[t], right[col], preferred_element_type=f32) for t, col, _, _ in work]
                images = [image.astype(jnp.bfloat16) for image in images]
                terms = [jnp.dot(left[w[2]], x, preferred_element_type=f32) for w, x in zip(work, images)]
                for w, term in zip(work, terms):
                    accum[w[3]] += term
                return carry

            steps = lax.div(jnp.maximum(count - done, 0) + unroll - smaller - 1, unroll)
            lax.fori_loop(0, steps, advance, 0)
            done = done + steps * unroll
        for out, start in zip(outs, parts):
            out[...] = accum[start : start + out.shape[0]].astype(out.dtype)


def coarse_chunk(pick, listed, blocks, outs, after=()):
    items, counts, a = listed
    held, width = blocks[0].shape[0], a.shape[1]
    chunk = 3 * held * (held if pick is None else 1)
    n_left = blocks[-1].shape[0] if pick is None else 4
    return pl.pallas_call(
        functools.partial(chunk_kernel, held, pick, len(blocks), [start for start, _, _ in outs]),
        out_shape=[jax.ShapeDtypeStruct((end - start, width, width), dtype) for start, end, dtype in outs],
        in_specs=[SMEM] * 2 + [VMEM] * (1 + len(blocks)) + [pl.BlockSpec(memory_space=pl.ANY)] * len(after),
        out_specs=[VMEM] * len(outs),
        scratch_shapes=[
            pltpu.VMEM((3 * held, width, width), jnp.bfloat16),
            pltpu.VMEM((n_left, width, width), jnp.bfloat16),
            pltpu.VMEM((chunk + 1, width, width), jnp.float32),
        ],
        compiler_params=pltpu.CompilerParams(vmem_limit_bytes=LIMIT),
        cost_estimate=pl.CostEstimate(flops=1 << 31, bytes_accessed=1 << 20, transcendentals=0),
        name="coarse_chunk",
    )(items, counts, a, *blocks, *after)


def mix_kernel(counts, x, y, z, *rest):
    out = rest[-1]
    me = counts[counts.shape[0] - 1]
    f32 = jnp.float32
    total = y[...].astype(f32) + z[...].astype(f32)
    out[...] = jnp.where((me == 0) | (me == 3), x[...].astype(f32), total).astype(out.dtype)


def mixed(counts, x, y, z, after=()):
    return pl.pallas_call(
        mix_kernel,
        out_shape=jax.ShapeDtypeStruct(x.shape, x.dtype),
        in_specs=[SMEM] + [VMEM] * 3 + [pl.BlockSpec(memory_space=pl.ANY)] * len(after),
        out_specs=VMEM,
        compiler_params=pltpu.CompilerParams(vmem_limit_bytes=LIMIT),
        name="mixed",
    )(counts, x, y, z, *after)


def most_kernel(counts, at_end, elsewhere, far, near, out):
    me = counts[counts.shape[0] - 1]
    end = (me == 0) | (me == 3)
    f32 = jnp.float32
    out[...] = jnp.where(end, at_end[...], elsewhere[...]) + jnp.where(end, far[...], near[...]).astype(f32)


def finish_kernel(most_a, most_b, got, out):
    half = most_a.shape[0]
    for i, most in enumerate((most_a, most_b)):
        part = slice(i * half, (i + 1) * half)
        out[part] = (most[...] + got[part].astype(jnp.float32)).astype(out.dtype)


def finished(counts, own, got, last):
    params = pltpu.CompilerParams(vmem_limit_bytes=LIMIT)
    most = [
        pl.pallas_call(
            most_kernel,
            out_shape=jax.ShapeDtypeStruct(x.shape, x.dtype),
            in_specs=[SMEM] + [VMEM] * 4,
            out_specs=VMEM,
            compiler_params=params,
            name="most",
        )(counts, x, y, far, near)
        for x, y, far, near in zip(*own, *got)
    ]
    return pl.pallas_call(
        finish_kernel,
        out_shape=jax.ShapeDtypeStruct(last.shape, last.dtype),
        in_specs=[VMEM] * 3,
        out_specs=VMEM,
        compiler_params=params,
        name="finished",
    )(*most, last)


def add_kernel(n, *refs):
    xs, out = refs[:n], refs[-1]
    total = xs[0][...]
    for x in xs[1:]:
        total = total.astype(jnp.float32) + x[...].astype(jnp.float32)
    out[...] = total.astype(out.dtype)


def added(xs, dtype, after=()):
    return pl.pallas_call(
        functools.partial(add_kernel, len(xs)),
        out_shape=jax.ShapeDtypeStruct(xs[0].shape, dtype),
        in_specs=[VMEM] * len(xs) + [pl.BlockSpec(memory_space=pl.ANY)] * len(after),
        out_specs=VMEM,
        compiler_params=pltpu.CompilerParams(vmem_limit_bytes=LIMIT),
        name="added",
    )(*xs, *after)


def shifted(block, axis, distance):
    n = lax.axis_size(axis)
    return lax.ppermute(block, axis, [((i - distance) % n, i) for i in range(n)])


def line_of_four(a_tiles, a_row, a_col, a_count, p_tiles):
    me = lax.axis_index("col").reshape(1)
    held, width = p_tiles.shape[:2]
    stay = lambda x: pltpu.with_memory_space_constraint(x, pltpu.HBM)
    a_tiles, a_row, a_col, p_tiles = stay(a_tiles), stay(a_row), stay(a_col), stay(p_tiles)
    cross = lambda block, pairs: lax.ppermute(block, "col", pairs)
    flips = [[(i, i ^ m) for i in range(4)] for m in range(4)]
    across = cross(p_tiles, [(2, 0), (1, 3), (0, 1), (3, 2)])
    beside = cross(p_tiles, [(1, 0), (2, 3), (0, 2), (3, 1)])
    opposite = cross(p_tiles, [(0, 3), (3, 0)])
    middle = cross(p_tiles, [(1, 2), (2, 1)])
    items, counts, a, own = plan(held, 4, me, a_row, a_col, a_count, a_tiles, p_tiles)
    below, above = shifted(p_tiles, "row", 1), shifted(p_tiles, "row", -1)
    part = dict(across=across, beside=beside, opposite=opposite, middle=middle, below=below, above=above)
    part = {name: pltpu.with_memory_space_constraint(x, pltpu.VMEM) for name, x in part.items()}
    part["own"] = own
    listed, blocks = (items, counts, a), [part[name] for name in PARTS]
    part["opposite"] = added([part["opposite"], part["middle"]], p_tiles.dtype)
    later = [part[name] for name in PARTS]

    bf16, f32 = jnp.bfloat16, jnp.float32
    chunk, half = 3 * held, 3 * held // 2
    cut = [(0, half), (half, chunk)]
    narrow, full = [(*c, bf16) for c in cut], [(*c, f32) for c in cut]
    ends, middles, over = [(0, 1), (3, 2)], [(1, 2), (2, 1)], [(1, 3), (2, 0)]
    part = lambda pick, outs, after=(): coarse_chunk(pick, listed, later, outs, after)
    (*first,) = coarse_chunk((3, -1, -1, 0), listed, blocks, narrow)
    got1 = cross(first[0], ends)
    *second, wide_a, wide_b = part((2, 3, 0, 1), narrow + full, first[:1])
    got2 = cross(added(first[1:], bf16, second[:1]), ends)
    sent3 = mixed(counts, second[0], wide_a, got1)
    got3 = cross(sent3, ends + over)
    sent4 = mixed(counts, second[1], wide_b, got2, [sent3])
    got4 = cross(sent4, ends + over)
    (third,) = part((1, 0, 3, 2), [(0, chunk, bf16)], [sent4])
    got5 = cross(third, flips[1])
    fourth = part((0, 2, 1, 3), full, [third])
    sent6 = added([fourth[0], got3], bf16, [third])
    got6 = cross(sent6, middles)
    sent7 = added([fourth[1], got4], bf16, [sent6])
    got7 = cross(sent7, middles)
    fifth = part((-1, 1, 2, -1), full, [sent7])
    return finished(counts, [fourth, fifth], [(got3, got4), (got6, got7)], got5)


def any_columns(a_tiles, a_row, a_col, a_count, p_tiles):
    n = lax.axis_size("col")
    held = p_tiles.shape[0]
    total = 3 * held * held
    rights = [shifted(p_tiles, "row", 1), p_tiles, shifted(p_tiles, "row", -1)]
    row_side = lax.all_gather(p_tiles, "col", axis=0, tiled=True)
    me = jnp.zeros((1,), jnp.int32)
    items, counts, a, own = plan(held, 1, me, a_row, a_col, a_count, a_tiles, p_tiles)
    blocks = (rights[0], own, rights[2], row_side)
    (sums,) = coarse_chunk(None, (items, counts, a), blocks, [(0, total, jnp.bfloat16)])
    parts = sums.reshape(n, total // n, *sums.shape[1:])
    parts = lax.all_to_all(parts, "col", 0, 0, tiled=True)
    return jnp.sum(parts.astype(jnp.float32), axis=0).astype(jnp.bfloat16)


def shards(a_tiles, a_row, a_col, a_count, p_tiles):
    special = lax.axis_size("col") == 4 and p_tiles.shape[0] == 4
    body = line_of_four if special else any_columns
    return body(a_tiles, a_row, a_col, a_count, p_tiles)


def solution(mesh):
    in_specs = (
        P(("row", "col"), None, None),
        P(("row", "col")),
        P(("row", "col")),
        P(("row", "col")),
        P(("row", "col"), None, None),
    )
    out_specs = P(("row", "col"), None, None)
    return jax.shard_map(shards, mesh=mesh, in_specs=in_specs, out_specs=out_specs, check_vma=False)
```

```python
import functools

import jax
import jax.numpy as jnp
from jax import lax
from jax.experimental import pallas as pl
from jax.experimental.pallas import tpu as pltpu
from jax.sharding import PartitionSpec as P

UNROLLS = (32, 16, 8, 4)
PARTS = ("opposite", "across", "beside", "below", "own", "above")
LIMIT = 12 * 1024 * 1024
VMEM = pl.BlockSpec(memory_space=pltpu.VMEM)
SMEM = pl.BlockSpec(memory_space=pltpu.SMEM)
HBM = pl.BlockSpec(memory_space=pltpu.HBM)


def bits(extent):
    return (extent - 1).bit_length()


def divide(x, n):
    if n & (n - 1):
        return lax.div(x, n), lax.rem(x, n)
    return x >> bits(n), x & (n - 1)


def plan_kernel(held, n, me, a_row, a_col, a_count, a, p, items, counts, a_out, p_out, sems):
    slots = a_row.shape[0]
    parts = sems.shape[0] - 1
    size = slots // parts
    copies = [pltpu.make_async_copy(p, p_out, sems.at[parts])]
    for i in range(parts):
        part = pl.ds(i * size, size)
        copies.append(pltpu.make_async_copy(a.at[part], a_out.at[part], sems.at[i]))
    for copy in copies:
        copy.start()
    field = 32 // n
    group = 8 if slots % 8 == 0 else 1
    live = a_count[0]

    def place(step, taken):
        for u in range(group):
            t = step * group + u
            row, col = a_row[t], a_col[t]
            d = divide(divide(row, held)[1] * n, held)[0]
            at = (taken >> (d * field)) & ((1 << min(field, 16)) - 1)
            items[d * slots + at] = t + (col << bits(slots)) + (row << (bits(slots) + bits(3 * held)))
            taken = taken + (jnp.where(t < live, 1, 0) << (d * field))
        return taken

    taken = lax.fori_loop(0, lax.div(live + group - 1, group), place, jnp.int32(0))
    for d in range(n):
        counts[d] = (taken >> (d * field)) & ((1 << min(field, 16)) - 1)
    counts[n] = me[0]
    for copy in copies:
        copy.wait()


def plan(held, n, me, a_row, a_col, a_count, a_tiles, p_tiles):
    return pl.pallas_call(
        functools.partial(plan_kernel, held, n),
        out_shape=(
            pltpu.SMEM((n * a_row.shape[0],), jnp.int32),
            pltpu.SMEM((n + 1,), jnp.int32),
            pltpu.VMEM(a_tiles.shape, a_tiles.dtype),
            pltpu.VMEM(p_tiles.shape, p_tiles.dtype),
        ),
        in_specs=[SMEM] * 4 + [HBM] * 2,
        out_specs=(SMEM, SMEM, VMEM, VMEM),
        scratch_shapes=[pltpu.SemaphoreType.DMA((5 if a_row.shape[0] % 4 == 0 else 2,))],
        compiler_params=pltpu.CompilerParams(vmem_limit_bytes=LIMIT),
        name="plan",
    )(me, a_row, a_col, a_count, a_tiles, p_tiles)


def chunk_kernel(held, pick, n_block, parts, items, counts, a, *rest):
    blocks, outs, (right, left, accum) = rest[:n_block], rest[-3 - len(parts) : -3], rest[-3:]
    slots, chunk = a.shape[0], accum.shape[0] - 1
    me = counts[counts.shape[0] - 1]
    d = 0 if pick is None else sum(jnp.where(me == i, x, 0) for i, x in enumerate(pick))

    @pl.when(d >= 0)
    def _():
        base, count = d * slots, counts[d]
        if pick is None:
            rights, rows = blocks[:3], blocks[3]
            for i in range(left.shape[0]):
                left[i] = rows[i].T
        else:
            part = dict(zip(PARTS, blocks))
            rights = part["below"], part["own"], part["above"]
            left[0] = part["own"][d].T
            end = (me == 0) | (me == 3)
            left[1] = jnp.where(end, part["beside"][d], part["across"][d]).T
            left[2] = jnp.where(end, part["across"][d], part["beside"][d]).T
            left[3] = part["opposite"][d].T
        for i, ref in enumerate(rights):
            right[i * held : (i + 1) * held] = ref[...]
        accum[...] = jnp.zeros_like(accum)

        def unpack(e):
            item = items[base + jnp.minimum(e, count - 1)]
            t, item = item & ((1 << bits(slots)) - 1), item >> bits(slots)
            col, row = item & ((1 << bits(3 * held)) - 1), item >> bits(3 * held)
            if pick is None:
                s = divide(row, held)[1] * (3 * held) + col
            else:
                row, s = divide(row, held)[0] ^ me, col
            return t, col, row, jnp.where(e < count, s, chunk)

        done = jnp.int32(0)
        for unroll, smaller in zip(UNROLLS, (*UNROLLS[1:], 0)):

            def advance(step, carry, done=done, unroll=unroll):
                work = [unpack(done + step * unroll + u) for u in range(unroll)]
                f32 = jnp.float32
                images = [jnp.dot(a[t], right[col], preferred_element_type=f32) for t, col, _, _ in work]
                images = [image.astype(jnp.bfloat16) for image in images]
                terms = [jnp.dot(left[w[2]], x, preferred_element_type=f32) for w, x in zip(work, images)]
                for w, term in zip(work, terms):
                    accum[w[3]] += term
                return carry

            steps = lax.div(jnp.maximum(count - done, 0) + unroll - smaller - 1, unroll)
            lax.fori_loop(0, steps, advance, 0)
            done = done + steps * unroll
        for out, start in zip(outs, parts):
            out[...] = accum[start : start + out.shape[0]].astype(out.dtype)


def coarse_chunk(pick, listed, blocks, outs, after=()):
    items, counts, a = listed
    held, width = blocks[0].shape[0], a.shape[1]
    chunk = 3 * held * (held if pick is None else 1)
    n_left = blocks[-1].shape[0] if pick is None else 4
    return pl.pallas_call(
        functools.partial(chunk_kernel, held, pick, len(blocks), [start for start, _, _ in outs]),
        out_shape=[jax.ShapeDtypeStruct((end - start, width, width), dtype) for start, end, dtype in outs],
        in_specs=[SMEM] * 2 + [VMEM] * (1 + len(blocks)) + [pl.BlockSpec(memory_space=pl.ANY)] * len(after),
        out_specs=[VMEM] * len(outs),
        scratch_shapes=[
            pltpu.VMEM((3 * held, width, width), jnp.bfloat16),
            pltpu.VMEM((n_left, width, width), jnp.bfloat16),
            pltpu.VMEM((chunk + 1, width, width), jnp.float32),
        ],
        compiler_params=pltpu.CompilerParams(vmem_limit_bytes=LIMIT),
        cost_estimate=pl.CostEstimate(flops=1 << 31, bytes_accessed=1 << 20, transcendentals=0),
        name="coarse_chunk",
    )(items, counts, a, *blocks, *after)


def mix_kernel(counts, x, y, z, *rest):
    out = rest[-1]
    me = counts[counts.shape[0] - 1]
    f32 = jnp.float32
    total = y[...].astype(f32) + z[...].astype(f32)
    out[...] = jnp.where((me == 0) | (me == 3), x[...].astype(f32), total).astype(out.dtype)


def mixed(counts, x, y, z, after=()):
    return pl.pallas_call(
        mix_kernel,
        out_shape=jax.ShapeDtypeStruct(x.shape, x.dtype),
        in_specs=[SMEM] + [VMEM] * 3 + [pl.BlockSpec(memory_space=pl.ANY)] * len(after),
        out_specs=VMEM,
        compiler_params=pltpu.CompilerParams(vmem_limit_bytes=LIMIT),
        name="mixed",
    )(counts, x, y, z, *after)


def most_kernel(counts, at_end, elsewhere, far, near, out):
    me = counts[counts.shape[0] - 1]
    end = (me == 0) | (me == 3)
    f32 = jnp.float32
    out[...] = jnp.where(end, at_end[...], elsewhere[...]) + jnp.where(end, far[...], near[...]).astype(f32)


def finish_kernel(most_a, most_b, got, out, total, sems):
    half, parts = most_a.shape[0], sems.shape[0]
    size = 2 * half // parts
    copies = []
    for i in range(parts):
        most, start = (most_a, i * size) if i * size < half else (most_b, i * size - half)
        part = slice(i * size, (i + 1) * size)
        total[part] = (most[start : start + size] + got[part].astype(jnp.float32)).astype(out.dtype)
        copies.append(pltpu.make_async_copy(total.at[part], out.at[part], sems.at[i]))
        copies[-1].start()
    for copy in copies:
        copy.wait()


def finished(counts, own, got, last):
    params = pltpu.CompilerParams(vmem_limit_bytes=LIMIT)
    most = [
        pl.pallas_call(
            most_kernel,
            out_shape=jax.ShapeDtypeStruct(x.shape, x.dtype),
            in_specs=[SMEM] + [VMEM] * 4,
            out_specs=VMEM,
            compiler_params=params,
            name="most",
        )(counts, x, y, far, near)
        for x, y, far, near in zip(*own, *got)
    ]
    return pl.pallas_call(
        finish_kernel,
        out_shape=jax.ShapeDtypeStruct(last.shape, last.dtype),
        in_specs=[VMEM] * 3,
        out_specs=HBM,
        scratch_shapes=[pltpu.VMEM(last.shape, last.dtype), pltpu.SemaphoreType.DMA((4,))],
        compiler_params=params,
        name="finished",
    )(*most, last)


def add_kernel(n, *refs):
    xs, out = refs[:n], refs[-1]
    total = xs[0][...]
    for x in xs[1:]:
        total = total.astype(jnp.float32) + x[...].astype(jnp.float32)
    out[...] = total.astype(out.dtype)


def added(xs, dtype, after=()):
    return pl.pallas_call(
        functools.partial(add_kernel, len(xs)),
        out_shape=jax.ShapeDtypeStruct(xs[0].shape, dtype),
        in_specs=[VMEM] * len(xs) + [pl.BlockSpec(memory_space=pl.ANY)] * len(after),
        out_specs=VMEM,
        compiler_params=pltpu.CompilerParams(vmem_limit_bytes=LIMIT),
        name="added",
    )(*xs, *after)


def shifted(block, axis, distance):
    n = lax.axis_size(axis)
    return lax.ppermute(block, axis, [((i - distance) % n, i) for i in range(n)])


def line_of_four(a_tiles, a_row, a_col, a_count, p_tiles):
    me = lax.axis_index("col").reshape(1)
    held, width = p_tiles.shape[:2]
    stay = lambda x: pltpu.with_memory_space_constraint(x, pltpu.HBM)
    a_tiles, a_row, a_col, p_tiles = stay(a_tiles), stay(a_row), stay(a_col), stay(p_tiles)
    cross = lambda block, pairs: lax.ppermute(block, "col", pairs)
    flips = [[(i, i ^ m) for i in range(4)] for m in range(4)]
    across = cross(p_tiles, [(2, 0), (1, 3), (0, 1), (3, 2)])
    beside = cross(p_tiles, [(1, 0), (2, 3), (0, 2), (3, 1)])
    opposite = cross(p_tiles, [(0, 3), (3, 0)])
    middle = cross(p_tiles, [(1, 2), (2, 1)])
    items, counts, a, own = plan(held, 4, me, a_row, a_col, a_count, a_tiles, p_tiles)
    below, above = shifted(p_tiles, "row", 1), shifted(p_tiles, "row", -1)
    part = dict(across=across, beside=beside, opposite=opposite, middle=middle, below=below, above=above)
    part = {name: pltpu.with_memory_space_constraint(x, pltpu.VMEM) for name, x in part.items()}
    part["own"] = own
    listed, blocks = (items, counts, a), [part[name] for name in PARTS]
    part["opposite"] = added([part["opposite"], part["middle"]], p_tiles.dtype)
    later = [part[name] for name in PARTS]

    bf16, f32 = jnp.bfloat16, jnp.float32
    chunk, half = 3 * held, 3 * held // 2
    cut = [(0, half), (half, chunk)]
    narrow, full = [(*c, bf16) for c in cut], [(*c, f32) for c in cut]
    ends, middles, over = [(0, 1), (3, 2)], [(1, 2), (2, 1)], [(1, 3), (2, 0)]
    part = lambda pick, outs, after=(): coarse_chunk(pick, listed, later, outs, after)
    (*first,) = coarse_chunk((3, -1, -1, 0), listed, blocks, narrow)
    got1 = cross(first[0], ends)
    *second, wide_a, wide_b = part((2, 3, 0, 1), narrow + full, first[:1])
    got2 = cross(added(first[1:], bf16, second[:1]), ends)
    sent3 = mixed(counts, second[0], wide_a, got1)
    got3 = cross(sent3, ends + over)
    sent4 = mixed(counts, second[1], wide_b, got2, [sent3])
    got4 = cross(sent4, ends + over)
    (third,) = part((1, 0, 3, 2), [(0, chunk, bf16)], [sent4])
    got5 = cross(third, flips[1])
    fourth = part((0, 2, 1, 3), full, [third])
    sent6 = added([fourth[0], got3], bf16, [third])
    got6 = cross(sent6, middles)
    sent7 = added([fourth[1], got4], bf16, [sent6])
    got7 = cross(sent7, middles)
    fifth = part((-1, 1, 2, -1), full, [sent7])
    return finished(counts, [fourth, fifth], [(got3, got4), (got6, got7)], got5)


def any_columns(a_tiles, a_row, a_col, a_count, p_tiles):
    n = lax.axis_size("col")
    held = p_tiles.shape[0]
    total = 3 * held * held
    rights = [shifted(p_tiles, "row", 1), p_tiles, shifted(p_tiles, "row", -1)]
    row_side = lax.all_gather(p_tiles, "col", axis=0, tiled=True)
    me = jnp.zeros((1,), jnp.int32)
    items, counts, a, own = plan(held, 1, me, a_row, a_col, a_count, a_tiles, p_tiles)
    blocks = (rights[0], own, rights[2], row_side)
    (sums,) = coarse_chunk(None, (items, counts, a), blocks, [(0, total, jnp.bfloat16)])
    parts = sums.reshape(n, total // n, *sums.shape[1:])
    parts = lax.all_to_all(parts, "col", 0, 0, tiled=True)
    return jnp.sum(parts.astype(jnp.float32), axis=0).astype(jnp.bfloat16)


def shards(a_tiles, a_row, a_col, a_count, p_tiles):
    special = lax.axis_size("col") == 4 and p_tiles.shape[0] == 4
    body = line_of_four if special else any_columns
    return body(a_tiles, a_row, a_col, a_count, p_tiles)


def solution(mesh):
    in_specs = (
        P(("row", "col"), None, None),
        P(("row", "col")),
        P(("row", "col")),
        P(("row", "col")),
        P(("row", "col"), None, None),
    )
    out_specs = P(("row", "col"), None, None)
    return jax.shard_map(shards, mesh=mesh, in_specs=in_specs, out_specs=out_specs, check_vma=False)
```

```python
import functools

import jax
import jax.numpy as jnp
from jax import lax
from jax.experimental import pallas as pl
from jax.experimental.pallas import tpu as pltpu
from jax.sharding import PartitionSpec as P

UNROLLS = (32, 8)
PARTS = ("opposite", "across", "beside", "below", "own", "above")
LIMIT = 12 * 1024 * 1024
VMEM = pl.BlockSpec(memory_space=pltpu.VMEM)
SMEM = pl.BlockSpec(memory_space=pltpu.SMEM)
HBM = pl.BlockSpec(memory_space=pltpu.HBM)


def bits(extent):
    return (extent - 1).bit_length()


def divide(x, n):
    if n & (n - 1):
        return lax.div(x, n), lax.rem(x, n)
    return x >> bits(n), x & (n - 1)


def plan_kernel(held, n, me, a_row, a_col, a_count, a, p, items, counts, a_out, p_out, sems):
    slots = a_row.shape[0]
    parts = sems.shape[0] - 1
    size = slots // parts
    copies = [pltpu.make_async_copy(p, p_out, sems.at[parts])]
    for i in range(parts):
        part = pl.ds(i * size, size)
        copies.append(pltpu.make_async_copy(a.at[part], a_out.at[part], sems.at[i]))
    for copy in copies:
        copy.start()
    field = 32 // n
    group = 8 if slots % 8 == 0 else 1
    live = a_count[0]

    def place(step, taken):
        for u in range(group):
            t = step * group + u
            row, col = a_row[t], a_col[t]
            d = divide(divide(row, held)[1] * n, held)[0]
            at = (taken >> (d * field)) & ((1 << min(field, 16)) - 1)
            items[d * slots + at] = t + (col << bits(slots)) + (row << (bits(slots) + bits(3 * held)))
            taken = taken + (jnp.where(t < live, 1, 0) << (d * field))
        return taken

    taken = lax.fori_loop(0, lax.div(live + group - 1, group), place, jnp.int32(0))
    for d in range(n):
        counts[d] = (taken >> (d * field)) & ((1 << min(field, 16)) - 1)
    counts[n] = me[0]
    for copy in copies:
        copy.wait()


def plan(held, n, me, a_row, a_col, a_count, a_tiles, p_tiles):
    return pl.pallas_call(
        functools.partial(plan_kernel, held, n),
        out_shape=(
            pltpu.SMEM((n * a_row.shape[0],), jnp.int32),
            pltpu.SMEM((n + 1,), jnp.int32),
            pltpu.VMEM(a_tiles.shape, a_tiles.dtype),
            pltpu.VMEM(p_tiles.shape, p_tiles.dtype),
        ),
        in_specs=[SMEM] * 4 + [HBM] * 2,
        out_specs=(SMEM, SMEM, VMEM, VMEM),
        scratch_shapes=[pltpu.SemaphoreType.DMA((5 if a_row.shape[0] % 4 == 0 else 2,))],
        compiler_params=pltpu.CompilerParams(vmem_limit_bytes=LIMIT),
        name="plan",
    )(me, a_row, a_col, a_count, a_tiles, p_tiles)


def chunk_kernel(held, pick, n_block, parts, items, counts, a, *rest):
    blocks, outs, (right, left, accum) = rest[:n_block], rest[-3 - len(parts) : -3], rest[-3:]
    slots, chunk = a.shape[0], accum.shape[0] - 1
    me = counts[counts.shape[0] - 1]
    d = 0 if pick is None else sum(jnp.where(me == i, x, 0) for i, x in enumerate(pick))

    @pl.when(d >= 0)
    def _():
        base, count = d * slots, counts[d]
        if pick is None:
            rights, rows = blocks[:3], blocks[3]
            for i in range(left.shape[0]):
                left[i] = rows[i].T
        else:
            part = dict(zip(PARTS, blocks))
            rights = part["below"], part["own"], part["above"]
            left[0] = part["own"][d].T
            end = (me == 0) | (me == 3)
            left[1] = jnp.where(end, part["beside"][d], part["across"][d]).T
            left[2] = jnp.where(end, part["across"][d], part["beside"][d]).T
            left[3] = part["opposite"][d].T
        for i, ref in enumerate(rights):
            right[i * held : (i + 1) * held] = ref[...]
        accum[...] = jnp.zeros_like(accum)

        def unpack(e):
            item = items[base + jnp.minimum(e, count - 1)]
            t, item = item & ((1 << bits(slots)) - 1), item >> bits(slots)
            col, row = item & ((1 << bits(3 * held)) - 1), item >> bits(3 * held)
            if pick is None:
                s = divide(row, held)[1] * (3 * held) + col
            else:
                row, s = divide(row, held)[0] ^ me, col
            return t, col, row, jnp.where(e < count, s, chunk)

        done = jnp.int32(0)
        for unroll, smaller in zip(UNROLLS, (*UNROLLS[1:], 0)):

            def advance(step, carry, done=done, unroll=unroll):
                work = [unpack(done + step * unroll + u) for u in range(unroll)]
                f32 = jnp.float32
                images = [jnp.dot(a[t], right[col], preferred_element_type=f32) for t, col, _, _ in work]
                images = [image.astype(jnp.bfloat16) for image in images]
                terms = [jnp.dot(left[w[2]], x, preferred_element_type=f32) for w, x in zip(work, images)]
                for w, term in zip(work, terms):
                    accum[w[3]] += term
                return carry

            steps = lax.div(jnp.maximum(count - done, 0) + unroll - smaller - 1, unroll)
            lax.fori_loop(0, steps, advance, 0)
            done = done + steps * unroll
        for out, start in zip(outs, parts):
            out[...] = accum[start : start + out.shape[0]].astype(out.dtype)


def coarse_chunk(pick, listed, blocks, outs, after=()):
    items, counts, a = listed
    held, width = blocks[0].shape[0], a.shape[1]
    chunk = 3 * held * (held if pick is None else 1)
    n_left = blocks[-1].shape[0] if pick is None else 4
    return pl.pallas_call(
        functools.partial(chunk_kernel, held, pick, len(blocks), [start for start, _, _ in outs]),
        out_shape=[jax.ShapeDtypeStruct((end - start, width, width), dtype) for start, end, dtype in outs],
        in_specs=[SMEM] * 2 + [VMEM] * (1 + len(blocks)) + [pl.BlockSpec(memory_space=pl.ANY)] * len(after),
        out_specs=[VMEM] * len(outs),
        scratch_shapes=[
            pltpu.VMEM((3 * held, width, width), jnp.bfloat16),
            pltpu.VMEM((n_left, width, width), jnp.bfloat16),
            pltpu.VMEM((chunk + 1, width, width), jnp.float32),
        ],
        compiler_params=pltpu.CompilerParams(vmem_limit_bytes=LIMIT),
        cost_estimate=pl.CostEstimate(flops=1 << 31, bytes_accessed=1 << 20, transcendentals=0),
        name="coarse_chunk",
    )(items, counts, a, *blocks, *after)


def mix_kernel(counts, x, y, z, *rest):
    out = rest[-1]
    me = counts[counts.shape[0] - 1]
    f32 = jnp.float32
    total = y[...].astype(f32) + z[...].astype(f32)
    out[...] = jnp.where((me == 0) | (me == 3), x[...].astype(f32), total).astype(out.dtype)


def mixed(counts, x, y, z, after=()):
    return pl.pallas_call(
        mix_kernel,
        out_shape=jax.ShapeDtypeStruct(x.shape, x.dtype),
        in_specs=[SMEM] + [VMEM] * 3 + [pl.BlockSpec(memory_space=pl.ANY)] * len(after),
        out_specs=VMEM,
        compiler_params=pltpu.CompilerParams(vmem_limit_bytes=LIMIT),
        name="mixed",
    )(counts, x, y, z, *after)


def most_kernel(counts, at_end, elsewhere, far, near, out):
    me = counts[counts.shape[0] - 1]
    end = (me == 0) | (me == 3)
    f32 = jnp.float32
    out[...] = jnp.where(end, at_end[...], elsewhere[...]) + jnp.where(end, far[...], near[...]).astype(f32)


def finish_kernel(most_a, most_b, got, out, total, sems):
    half, parts = most_a.shape[0], sems.shape[0]
    size = 2 * half // parts
    copies = []
    for i in range(parts):
        most, start = (most_a, i * size) if i * size < half else (most_b, i * size - half)
        part = slice(i * size, (i + 1) * size)
        total[part] = (most[start : start + size] + got[part].astype(jnp.float32)).astype(out.dtype)
        copies.append(pltpu.make_async_copy(total.at[part], out.at[part], sems.at[i]))
        copies[-1].start()
    for copy in copies:
        copy.wait()


def finished(counts, own, got, last):
    params = pltpu.CompilerParams(vmem_limit_bytes=LIMIT)
    most = [
        pl.pallas_call(
            most_kernel,
            out_shape=jax.ShapeDtypeStruct(x.shape, x.dtype),
            in_specs=[SMEM] + [VMEM] * 4,
            out_specs=VMEM,
            compiler_params=params,
            name="most",
        )(counts, x, y, far, near)
        for x, y, far, near in zip(*own, *got)
    ]
    return pl.pallas_call(
        finish_kernel,
        out_shape=jax.ShapeDtypeStruct(last.shape, last.dtype),
        in_specs=[VMEM] * 3,
        out_specs=HBM,
        scratch_shapes=[pltpu.VMEM(last.shape, last.dtype), pltpu.SemaphoreType.DMA((4,))],
        compiler_params=params,
        name="finished",
    )(*most, last)


def add_kernel(n, *refs):
    xs, out = refs[:n], refs[-1]
    total = xs[0][...]
    for x in xs[1:]:
        total = total.astype(jnp.float32) + x[...].astype(jnp.float32)
    out[...] = total.astype(out.dtype)


def added(xs, dtype, after=()):
    return pl.pallas_call(
        functools.partial(add_kernel, len(xs)),
        out_shape=jax.ShapeDtypeStruct(xs[0].shape, dtype),
        in_specs=[VMEM] * len(xs) + [pl.BlockSpec(memory_space=pl.ANY)] * len(after),
        out_specs=VMEM,
        compiler_params=pltpu.CompilerParams(vmem_limit_bytes=LIMIT),
        name="added",
    )(*xs, *after)


def shifted(block, axis, distance):
    n = lax.axis_size(axis)
    return lax.ppermute(block, axis, [((i - distance) % n, i) for i in range(n)])


def line_of_four(a_tiles, a_row, a_col, a_count, p_tiles):
    me = lax.axis_index("col").reshape(1)
    held, width = p_tiles.shape[:2]
    stay = lambda x: pltpu.with_memory_space_constraint(x, pltpu.HBM)
    a_tiles, a_row, a_col, p_tiles = stay(a_tiles), stay(a_row), stay(a_col), stay(p_tiles)
    cross = lambda block, pairs: lax.ppermute(block, "col", pairs)
    flips = [[(i, i ^ m) for i in range(4)] for m in range(4)]
    across = cross(p_tiles, [(2, 0), (1, 3), (0, 1), (3, 2)])
    beside = cross(p_tiles, [(1, 0), (2, 3), (0, 2), (3, 1)])
    opposite = cross(p_tiles, [(0, 3), (3, 0)])
    middle = cross(p_tiles, [(1, 2), (2, 1)])
    items, counts, a, own = plan(held, 4, me, a_row, a_col, a_count, a_tiles, p_tiles)
    below, above = shifted(p_tiles, "row", 1), shifted(p_tiles, "row", -1)
    part = dict(across=across, beside=beside, opposite=opposite, middle=middle, below=below, above=above)
    part = {name: pltpu.with_memory_space_constraint(x, pltpu.VMEM) for name, x in part.items()}
    part["own"] = own
    listed, blocks = (items, counts, a), [part[name] for name in PARTS]
    part["opposite"] = added([part["opposite"], part["middle"]], p_tiles.dtype)
    later = [part[name] for name in PARTS]

    bf16, f32 = jnp.bfloat16, jnp.float32
    chunk, half = 3 * held, 3 * held // 2
    cut = [(0, half), (half, chunk)]
    narrow, full = [(*c, bf16) for c in cut], [(*c, f32) for c in cut]
    ends, middles, over = [(0, 1), (3, 2)], [(1, 2), (2, 1)], [(1, 3), (2, 0)]
    part = lambda pick, outs, after=(): coarse_chunk(pick, listed, later, outs, after)
    (*first,) = coarse_chunk((3, -1, -1, 0), listed, blocks, narrow)
    got1 = cross(first[0], ends)
    *second, wide_a, wide_b = part((2, 3, 0, 1), narrow + full, first[:1])
    got2 = cross(added(first[1:], bf16, second[:1]), ends)
    sent3 = mixed(counts, second[0], wide_a, got1)
    got3 = cross(sent3, ends + over)
    sent4 = mixed(counts, second[1], wide_b, got2, [sent3])
    got4 = cross(sent4, ends + over)
    (third,) = part((1, 0, 3, 2), [(0, chunk, bf16)], [sent4])
    got5 = cross(third, flips[1])
    fourth = part((0, 2, 1, 3), full, [third])
    sent6 = added([fourth[0], got3], bf16, [third])
    got6 = cross(sent6, middles)
    sent7 = added([fourth[1], got4], bf16, [sent6])
    got7 = cross(sent7, middles)
    fifth = part((-1, 1, 2, -1), full, [sent7])
    return finished(counts, [fourth, fifth], [(got3, got4), (got6, got7)], got5)


def any_columns(a_tiles, a_row, a_col, a_count, p_tiles):
    n = lax.axis_size("col")
    held = p_tiles.shape[0]
    total = 3 * held * held
    rights = [shifted(p_tiles, "row", 1), p_tiles, shifted(p_tiles, "row", -1)]
    row_side = lax.all_gather(p_tiles, "col", axis=0, tiled=True)
    me = jnp.zeros((1,), jnp.int32)
    items, counts, a, own = plan(held, 1, me, a_row, a_col, a_count, a_tiles, p_tiles)
    blocks = (rights[0], own, rights[2], row_side)
    (sums,) = coarse_chunk(None, (items, counts, a), blocks, [(0, total, jnp.bfloat16)])
    parts = sums.reshape(n, total // n, *sums.shape[1:])
    parts = lax.all_to_all(parts, "col", 0, 0, tiled=True)
    return jnp.sum(parts.astype(jnp.float32), axis=0).astype(jnp.bfloat16)


def shards(a_tiles, a_row, a_col, a_count, p_tiles):
    special = lax.axis_size("col") == 4 and p_tiles.shape[0] == 4
    body = line_of_four if special else any_columns
    return body(a_tiles, a_row, a_col, a_count, p_tiles)


def solution(mesh):
    in_specs = (
        P(("row", "col"), None, None),
        P(("row", "col")),
        P(("row", "col")),
        P(("row", "col")),
        P(("row", "col"), None, None),
    )
    out_specs = P(("row", "col"), None, None)
    return jax.shard_map(shards, mesh=mesh, in_specs=in_specs, out_specs=out_specs, check_vma=False)
```
